512 devices in a mesh: pipe: 16 (over y, x), tp: 32 (over z, core).
Axes of the slice: x: 4, y: 4, z: 16, core: 2. Of those that a mesh axis runs over, the one named last changes fastest.
Arguments:
- x_saved: bfloat16 [16, 128, 8192], P('pipe', None, 'tp'), may hold values from -8 to 8
- gains: float32 [16, 8192], P('pipe', 'tp'), may hold values from 0.1 to 1.9
- w_blocks: bfloat16 [16, 2304, 128, 128], P('pipe', 'tp')
- slot_pos: int32 [16, 2304], P('pipe', 'tp'), may hold values from 0 to 4095, as said below
- slot_live: int32 [16, 2304], P('pipe', 'tp'), may hold values from 0 to 1, as said below
- kl_grads: bfloat16 [2, 128, 8192], P(None, None, 'tp')
- teacher: int32 [128], replicated, may hold values 0 or 1
Outputs:
- w_grads: bfloat16 [16, 2304, 128, 128], P('pipe', 'tp')
- gain_grads: float32 [16, 8192], P('pipe', 'tp')
The draws below stay inside these ranges and needn't reach their ends.
Inputs may be any that keep to these rules, and one draw needn't show every extreme that they name: `slot_pos`: each slot's block index row_block * 64 + col_block. The slots held by tp device t lie in its own row blocks t * 2 to (t + 1) * 2 - 1, and within a layer all positions are distinct. Every layer holds each block whose row block equals its column block. `slot_live`: in each layer every tp device holds from 56 to 72 live slots, and one device holds exactly 72. The slots of blocks whose row block equals their column block are live.
All inputs are finite; a program needn't handle non-finite values.
Results may differ from the reference program's by a relative error of at most 0.012.
Values may be sent and summed in bfloat16 or wider, within the bound.
No kernel may reach another device: no remote copies, remote signals or barrier semaphores. Data moves between devices by JAX's collectives and lax.ppermute only.
A program may use at most 64 MiB of HBM per device.

```python
import jax
import jax.numpy as jnp
from jax import lax

D = 8192
BLK = 128
TOK = 128
SECTIONS = 16
NBC = 64
RB_DEV = 2
CAP = 72
SLOTS = 2304
N_TP = 32


diagonal_lift = 0.08


input_scale = 0.7


lower_size = 0.5


upper_size = 2.0


def swap_front(order, value, place):
    where_now = jnp.argmax(order == value).astype(jnp.int32)
    moved = order[place]
    order = order.at[where_now].set(moved)
    return order.at[place].set(value)


def slot_layout(key):
    local_count = RB_DEV * NBC
    order_keys = jax.random.split(jax.random.fold_in(key, 11), SECTIONS * N_TP)
    device_ids = jnp.tile(jnp.arange(N_TP, dtype=jnp.int32), SECTIONS)

    def one_order(sub_key, device):
        order = jax.random.permutation(sub_key, local_count).astype(jnp.int32)
        for row in range(RB_DEV):
            order = swap_front(order, row * NBC + device * RB_DEV + row, row)
        return order
    orders = jax.vmap(one_order)(order_keys, device_ids)
    orders = orders.reshape(SECTIONS, N_TP, local_count)[:, :, :CAP].astype(jnp.int32)
    offsets = (jnp.arange(N_TP, dtype=jnp.int32) * local_count)[None, :, None]
    positions = orders + offsets
    count_key = jax.random.fold_in(key, 12)
    fullest_key = jax.random.fold_in(key, 13)
    rank_key = jax.random.fold_in(key, 14)
    counts = jax.random.randint(count_key, (SECTIONS, N_TP), CAP * 7 // 9, CAP + 1)
    fullest = jax.random.randint(fullest_key, (SECTIONS,), 0, N_TP)
    counts = jnp.where(jnp.arange(N_TP)[None, :] == fullest[:, None], CAP, counts)
    rank_keys = jax.random.split(rank_key, SECTIONS * N_TP)
    rest = jax.vmap(lambda sub_key: jax.random.permutation(sub_key, CAP - RB_DEV))(rank_keys)
    rest = rest.reshape(SECTIONS, N_TP, CAP - RB_DEV).astype(jnp.int32) + RB_DEV
    front = jnp.broadcast_to(jnp.arange(RB_DEV, dtype=jnp.int32)[None, None, :], (SECTIONS, N_TP, RB_DEV))
    ranks = jnp.concatenate([front, rest], axis=2)
    live_slot = (ranks < counts[:, :, None]).astype(jnp.int32)
    return (positions.reshape(SECTIONS, N_TP * CAP), live_slot.reshape(SECTIONS, N_TP * CAP))


def shared_rows(key):
    return jax.random.normal(key, (TOK, D), jnp.float32)


def draw_slot_pos(key, part):
    return slot_layout(key)[0]


def draw_slot_live(key, part):
    return slot_layout(key)[1]


def draw_x_saved(key, part):
    common = shared_rows(key)
    key = jax.random.fold_in(key, 21)
    feature_pos = jnp.arange(D, dtype=jnp.float32) / (D - 1)
    noise = jax.random.normal(key, (SECTIONS, TOK, D), jnp.float32)
    ramp = 0.5 + 2.0 * feature_pos
    field = input_scale * (ramp[None, None, :] * common[None, :, :] + noise)
    return jnp.clip(field, -8.0, 8.0).astype(jnp.bfloat16)


def draw_kl_grads(key, part):
    common = shared_rows(key)
    key = jax.random.fold_in(key, 22)
    sign_key = jax.random.fold_in(key, 31)
    magnitude_key = jax.random.fold_in(key, 32)
    group_width = 2 * BLK
    group_count = D // group_width
    sign_field = jnp.where(jax.random.bernoulli(sign_key, 0.5, (2, TOK, group_count)), 1.0, -1.0).astype(jnp.float32)
    magnitude = jnp.exp(jax.random.uniform(magnitude_key, (2, TOK, group_count), jnp.float32, jnp.log(lower_size), jnp.log(upper_size)))
    private = jax.random.normal(key, (2, TOK, D), jnp.float32)
    scaling = jnp.repeat(sign_field * magnitude, group_width, axis=2, total_repeat_length=D)
    return (0.125 * (0.9 * scaling * common[None, :, :] + 0.45 * private)).astype(jnp.bfloat16)


def draw_w_blocks(key, part):
    key = jax.random.fold_in(key, 23)
    spread = (8.0 * D) ** (-0.5)
    noise = jax.random.normal(key, (SECTIONS, SLOTS, BLK, BLK), jnp.float32)
    diag_slot = (jnp.arange(SLOTS, dtype=jnp.int32) % CAP < RB_DEV).astype(jnp.float32)
    identity = (jnp.arange(BLK)[:, None] == jnp.arange(BLK)[None, :]).astype(jnp.float32)
    lifted = diagonal_lift * diag_slot[None, :, None, None] * identity[None, None, :, :]
    return (noise * spread + lifted).astype(jnp.bfloat16)


def place_ends(drawn, key, smallest, top_value):
    spot = [jax.random.randint(jax.random.fold_in(key, axis), (), 0, length) for axis, length in enumerate(drawn.shape)]
    widest = drawn.shape.index(max(drawn.shape))
    neighbour = spot[:widest] + [(spot[widest] + 1) % drawn.shape[widest]] + spot[widest + 1:]
    return drawn.at[tuple(spot)].set(smallest).at[tuple(neighbour)].set(top_value)


def setup_inputs(seed: int = 0) -> dict:
    keys = jax.random.split(jax.random.key(seed), 8)
    return {
        "x_saved": draw_x_saved(jax.random.fold_in(keys[7], 71), 0),
        "gains": jnp.clip(1.0 + 0.18 * jax.random.normal(keys[1], (SECTIONS, D), jnp.float32), 0.1, 1.9),
        "w_blocks": draw_w_blocks(jax.random.fold_in(keys[7], 71), 0),
        "slot_pos": draw_slot_pos(jax.random.fold_in(keys[7], 71), 0),
        "slot_live": draw_slot_live(jax.random.fold_in(keys[7], 71), 0),
        "kl_grads": draw_kl_grads(jax.random.fold_in(keys[7], 71), 0),
        "teacher": place_ends((jax.random.randint(keys[6], (TOK,), 0, 2) < 1).astype(jnp.int32), jax.random.fold_in(keys[6], 1), 0, 1),
    }


norm_epsilon = 1e-05

def reference(x_saved, gains, w_blocks, slot_pos, slot_live, kl_grads, teacher):
    col_count = D // BLK
    entry_grads = jnp.where((teacher == 1)[:, None], kl_grads[1], kl_grads[0])

    def section_back(grad_out, packed):
        inputs, gain_row, blocks, positions, live_slot = packed
        x_rows = inputs.astype(jnp.float32)
        inv_rms = lax.rsqrt(lax.optimization_barrier(jnp.mean(x_rows * x_rows, axis=1)) + norm_epsilon)
        unit_rows = x_rows * inv_rms[:, None]
        normed = (unit_rows * gain_row).astype(jnp.bfloat16)
        row_of = positions // col_count
        col_of = positions % col_count
        kept_blocks = blocks * live_slot[:, None, None].astype(blocks.dtype)
        picked = grad_out.reshape(TOK, col_count, BLK)[:, col_of, :].astype(jnp.float32)
        block_terms = jnp.einsum('tkb,kab->kta', picked, kept_blocks.astype(jnp.float32))
        summed = jax.ops.segment_sum(block_terms, row_of, num_segments=col_count)
        normed_grad = jnp.moveaxis(summed, 0, 1).reshape(TOK, D)
        scaled_dn = gain_row * normed_grad
        dot_sums = lax.optimization_barrier(jnp.sum(scaled_dn * unit_rows, axis=1))
        input_grad = grad_out.astype(jnp.float32) + inv_rms[:, None] * (scaled_dn - unit_rows * (dot_sums / D)[:, None])
        gain_grad = lax.optimization_barrier(jnp.sum(normed_grad * unit_rows, axis=0))
        left_rows = normed.reshape(TOK, col_count, BLK)[:, row_of, :].astype(jnp.float32)
        right_rows = grad_out.reshape(TOK, col_count, BLK)[:, col_of, :].astype(jnp.float32)
        slot_grads = jnp.einsum('tka,tkb->kab', left_rows, right_rows) * live_slot[:, None, None].astype(jnp.float32)
        return (input_grad.astype(jnp.bfloat16), (slot_grads.astype(jnp.bfloat16), gain_grad))
    final_grad, outputs = lax.scan(section_back, entry_grads, (x_saved, gains, w_blocks, slot_pos, slot_live), reverse=True)
    return (outputs[0], outputs[1])
```

```python
import functools

import jax
import jax.numpy as jnp
from jax import lax
from jax.experimental import pallas as pl
from jax.experimental.pallas import tpu as pltpu
from jax.sharding import PartitionSpec as P

norm_epsilon = 1e-05
group = 4
lanes = 128
f32 = jnp.float32
bf16 = jnp.bfloat16
across_last = (((1,), (1,)), ((), ()))


def params(mebibytes):
    return pltpu.CompilerParams(vmem_limit_bytes=mebibytes << 20)


def expand_body(code_ref, blocks_ref, dense_ref, *, col_blocks):
    slots, size = blocks_ref.shape[0], blocks_ref.shape[1]
    dead = 2 * col_blocks
    dense_ref[...] = jnp.zeros_like(dense_ref)

    def place(slot, carry):
        code = code_ref[slot]

        @pl.when(code < dead)
        def _():
            row, col = code // col_blocks, code % col_blocks
            rows = pl.ds(pl.multiple_of(row * size, size), size)
            cols = pl.ds(pl.multiple_of((col % 2) * size, size), size)
            dense_ref[col // 2, rows, cols] = blocks_ref[slot]

        return carry

    lax.fori_loop(0, slots, place, 0)


def expand(codes, blocks, shards):
    width = 2 * blocks.shape[1]
    return pl.pallas_call(
        functools.partial(expand_body, col_blocks=2 * shards),
        out_shape=jax.ShapeDtypeStruct((shards, width, width), bf16),
        in_specs=[
            pl.BlockSpec(memory_space=pltpu.SMEM),
            pl.BlockSpec(memory_space=pltpu.VMEM),
        ],
        out_specs=pl.BlockSpec(memory_space=pltpu.VMEM),
        compiler_params=params(24),
        name="expand",
    )(codes, blocks)


def layer_body(
    gathered, tails, own, above, above_own, above_scale, weight, here, inv_rms, gain,
    full_out, sent_out, own_out, total, shift,
):
    step, last = pl.program_id(0), pl.num_programs(0) - 1
    width = weight.shape[1]

    @pl.when(step == 0)
    def _():
        dots = jnp.sum(jnp.sum(tails[...].astype(f32), axis=0), axis=1, keepdims=True)
        shift[...] = jnp.broadcast_to(above_scale[...] * dots, shift.shape)
        total[...] = jnp.zeros_like(total)

    factor = shift[:, :1]
    acc = total[...]
    for i in range(gathered.shape[0]):
        piece = gathered[i, :, :width].astype(f32) - factor * above[i].astype(f32)
        piece = piece.astype(bf16)
        full_out[i] = piece
        acc += lax.dot_general(piece, weight[i], across_last, preferred_element_type=f32)
    total[...] = acc

    @pl.when(step == last)
    def _():
        grad = own[...] - factor * above_own[...].astype(f32)
        scaled = gain[...] * acc
        rms = inv_rms[...]
        dots = jnp.sum(scaled * (here[...].astype(f32) * rms), axis=1, keepdims=True)
        result = grad + rms * scaled
        own_out[...] = result
        sent_out[:, :width] = result.astype(bf16)
        high = dots.astype(bf16).astype(f32)
        low = (dots - high).astype(bf16).astype(f32)
        lane = lax.broadcasted_iota(jnp.int32, (dots.shape[0], lanes), 1)
        tail = jnp.where(lane == 0, high, jnp.where(lane == 1, low, 0.0))
        sent_out[:, width:] = tail.astype(bf16)


def layer(gathered, own, above, above_at, above_own, above_scale, weight, here, inv_rms, gain):
    shards, tokens, wide = gathered.shape
    width = wide - lanes
    chunk = min(8, shards)

    def whole(*shape):
        return pl.BlockSpec(shape, lambda c: (0,) * len(shape))

    return pl.pallas_call(
        layer_body,
        grid=(shards // chunk,),
        out_shape=(
            jax.ShapeDtypeStruct((shards, tokens, width), bf16),
            jax.ShapeDtypeStruct((tokens, wide), bf16),
            jax.ShapeDtypeStruct((tokens, width), f32),
        ),
        in_specs=[
            pl.BlockSpec((chunk, tokens, wide), lambda c: (c, 0, 0)),
            pl.BlockSpec((shards, tokens, lanes), lambda c: (0, 0, width // lanes)),
            whole(tokens, width),
            pl.BlockSpec((chunk, tokens, width), lambda c: (c, above_at, 0)),
            whole(tokens, width),
            whole(tokens, 1),
            pl.BlockSpec((chunk, width, width), lambda c: (c, 0, 0)),
            whole(tokens, width),
            whole(tokens, 1),
            whole(1, width),
        ],
        out_specs=(
            pl.BlockSpec((chunk, tokens, width), lambda c: (c, 0, 0)),
            whole(tokens, wide),
            whole(tokens, width),
        ),
        scratch_shapes=[pltpu.VMEM((tokens, width), f32), pltpu.VMEM((tokens, lanes), f32)],
        compiler_params=params(16),
        name="layer",
    )(gathered, gathered, own, above, above_own, above_scale, weight, here, inv_rms, gain)


def grads_body(code_ref, came, inputs, gain, blocks, out, gain_out, right, left, totals, *, col_blocks):
    size = blocks.shape[1]
    shards, part = came.shape[1] - 1, came.shape[2]
    rms = []
    for x in range(group):
        rms.append(jnp.sum(came[x, shards].astype(f32), axis=1, keepdims=True))
    rms = jnp.concatenate(rms, axis=0)
    normed = (inputs[...].astype(f32) * rms * gain[...]).astype(bf16).astype(f32)
    for row in range(2):
        left[row] = normed[:, row * size:(row + 1) * size].T.astype(bf16)
        totals[row] = jnp.zeros_like(totals[row])

    def arrange(shard, carry):
        for x in range(group):
            rows = slice(x * part, (x + 1) * part)
            right[2 * shard, rows, :] = came[x, shard, :, :size]
            right[2 * shard + 1, rows, :] = came[x, shard, :, size:]
        return carry

    lax.fori_loop(0, shards, arrange, 0)
    dead = 2 * col_blocks

    def one(slot, carry):
        code = code_ref[slot]
        live = (code < dead).astype(f32)
        place = code % dead
        row, col = place // col_blocks, place % col_blocks
        grad = jnp.dot(left[row], right[col], preferred_element_type=f32) * live
        out[slot] = grad.astype(bf16)
        totals[row] += grad * blocks[slot].astype(f32)
        return carry

    lax.fori_loop(0, blocks.shape[0], one, 0)
    for row in range(2):
        gain_out[row * size:(row + 1) * size, :] = jnp.sum(totals[row], axis=1, keepdims=True)


def slot_grads(codes, came, inputs, gain, blocks):
    slots, size = blocks.shape[0], blocks.shape[1]
    tokens, width = inputs.shape
    shards = came.shape[1] - 1
    vmem = pl.BlockSpec(memory_space=pltpu.VMEM)
    return pl.pallas_call(
        functools.partial(grads_body, col_blocks=2 * shards),
        out_shape=(
            jax.ShapeDtypeStruct(blocks.shape, bf16),
            jax.ShapeDtypeStruct((width, 1), f32),
        ),
        in_specs=[pl.BlockSpec(memory_space=pltpu.SMEM)] + [vmem] * 4,
        out_specs=(vmem, vmem),
        scratch_shapes=[
            pltpu.VMEM((2 * shards, tokens, size), bf16),
            pltpu.VMEM((2, size, tokens), bf16),
            pltpu.VMEM((2, size, size), f32),
        ],
        compiler_params=params(32),
        name="slot_grads",
    )(codes, came, inputs, gain, blocks)


def in_parts(value):
    parts = []
    for _ in range(3):
        part = lax.reduce_precision(value, 8, 7)
        parts.append(part.astype(bf16))
        value = value - part
    return parts


def per_device(x_saved, gains, w_blocks, slot_pos, slot_live, kl_grads, teacher):
    sections, shards = lax.axis_size("pipe"), lax.axis_size("tp")
    section, shard = lax.axis_index("pipe"), lax.axis_index("tp")
    line, block = section // group, section % group
    lines = sections // group
    together = [[i * group + x for x in range(group)] for i in range(lines)]
    down = [(i, i - group) for i in range(group, sections)]
    tokens, width = x_saved.shape[1], x_saved.shape[2]
    part = tokens // group
    full_width = width * shards
    blocks = w_blocks[0]
    slots = blocks.shape[0]
    places = 4 * shards
    codes = slot_pos[0] - shard * places + places * (1 - slot_live[0])

    weights = lax.all_gather(blocks, "pipe", axis_index_groups=together)
    code_row = jnp.zeros((width,), f32).at[:slots].set(codes.astype(f32)).astype(bf16)
    notes = jnp.stack(in_parts(gains[0]) + [code_row])
    notes = jnp.concatenate([notes, jnp.zeros((12, width), bf16)])
    notes = jnp.broadcast_to(notes[None], (group,) + notes.shape)
    told = jnp.concatenate([x_saved[0].reshape(group, part, width), notes], axis=1)
    told = lax.all_to_all(told, "pipe", 0, 0, axis_index_groups=together)
    inputs = told[:, :part]
    gain_rows = jnp.sum(told[:, part:part + 3].astype(f32), axis=1)
    line_codes = told[:, part + 3, :slots].astype(jnp.int32)

    all_inputs = lax.all_gather(inputs.reshape(tokens, width), "tp")
    squares = jnp.sum(jnp.square(all_inputs.astype(f32)), axis=(0, 2))
    inv_rms = lax.rsqrt(squares / full_width + norm_epsilon).reshape(group, part, 1)
    correct = jnp.square(inv_rms) / full_width
    upper = lax.ppermute(all_inputs[:, :part], "pipe", down)
    upper_squares = jnp.sum(jnp.square(upper.astype(f32)), axis=(0, 2))
    upper_correct = (1.0 / (upper_squares / full_width + norm_epsilon) / full_width)[:, None]
    upper_own = lax.dynamic_index_in_dim(upper, shard, 0, keepdims=False)

    entry = jnp.where((teacher == 1)[:, None], kl_grads[1], kl_grads[0])
    entry = lax.dynamic_slice_in_dim(entry, block * part, part, 0)
    sent = jnp.concatenate([entry, jnp.zeros((part, lanes), bf16)], axis=1)
    own = entry.astype(f32)

    dense = [None] * group
    kept = [None] * group
    for step in range(sections):
        phase, place = step // group, group - 1 - step % group
        if phase == 0:
            dense[place] = expand(line_codes[place], weights[place], shards)
        if step == 0:
            above, above_at, above_own = all_inputs, 0, inputs[0]
            scale = jnp.zeros((part, 1), f32)
        elif place == group - 1:
            passed = jnp.concatenate([own, sent[:, width:].astype(f32)], axis=1)
            passed = lax.ppermute(passed, "pipe", down)
            own, sent = passed[:, :width], passed.astype(bf16)
            above, above_at, above_own, scale = upper, 0, upper_own, upper_correct
        else:
            above, above_at = all_inputs, place + 1
            above_own, scale = inputs[place + 1], correct[place + 1]
        gathered = lax.all_gather(sent, "tp")
        full, sent, own = layer(
            gathered, own, above, above_at, above_own, scale, dense[place],
            inputs[place], inv_rms[place], gain_rows[place][None],
        )
        if phase == 0:
            kept[place] = full
        else:
            kept[place] = jnp.where(line == lines - 1 - phase, full, kept[place])

    rms_parts = jnp.concatenate(in_parts(inv_rms), axis=2)
    rms_parts = jnp.pad(rms_parts, ((0, 0), (0, 0), (0, width - 3)))
    came = jnp.concatenate([jnp.stack(kept), rms_parts[:, None]], axis=1)
    came = lax.all_to_all(came, "pipe", 0, 0, axis_index_groups=together)
    w_grads, gain_sums = slot_grads(codes, came, x_saved[0], gains, blocks)
    return (w_grads[None], gain_sums.reshape(1, width) / gains)


def solution(mesh):
    in_specs = (
        P("pipe", None, "tp"),
        P("pipe", "tp"),
        P("pipe", "tp", None, None),
        P("pipe", "tp"),
        P("pipe", "tp"),
        P(None, None, "tp"),
        P(),
    )
    out_specs = (P("pipe", "tp", None, None), P("pipe", "tp"))
    return jax.shard_map(
        per_device, mesh=mesh, in_specs=in_specs, out_specs=out_specs, check_vma=False
    )
```

```python
import functools

import jax
import jax.numpy as jnp
from jax import lax
from jax.experimental import pallas as pl
from jax.experimental.pallas import tpu as pltpu
from jax.sharding import PartitionSpec as P

norm_epsilon = 1e-05
group = 4
lanes = 128
f32 = jnp.float32
bf16 = jnp.bfloat16
across_last = (((1,), (1,)), ((), ()))


def params(mebibytes):
    return pltpu.CompilerParams(vmem_limit_bytes=mebibytes << 20)


def expand_body(code_ref, from_ref, mine, near, far, wrap, dense_ref, blocks, arrival, *, col_blocks):
    slots, size = blocks.shape[0], blocks.shape[1]
    dead = 2 * col_blocks
    for distance, source in enumerate((mine, near, far, wrap)):

        @pl.when(from_ref[0] == distance)
        def _():
            pltpu.make_async_copy(source, blocks, arrival.at[distance]).start()

    dense_ref[...] = jnp.zeros_like(dense_ref)
    for distance, source in enumerate((mine, near, far, wrap)):

        @pl.when(from_ref[0] == distance)
        def _():
            pltpu.make_async_copy(source, blocks, arrival.at[distance]).wait()

    def place(slot, carry):
        code = code_ref[slot]

        @pl.when(code < dead)
        def _():
            row, col = code // col_blocks, code % col_blocks
            rows = pl.ds(pl.multiple_of(row * size, size), size)
            cols = pl.ds(pl.multiple_of((col % 2) * size, size), size)
            dense_ref[col // 2, rows, cols] = blocks[slot]

        return carry

    lax.fori_loop(0, slots, place, 0)


def expand(codes, distance, copies, shards):
    width = 2 * copies[0].shape[1]
    smem = pl.BlockSpec(memory_space=pltpu.SMEM)
    return pl.pallas_call(
        functools.partial(expand_body, col_blocks=2 * shards),
        out_shape=jax.ShapeDtypeStruct((shards, width, width), bf16),
        in_specs=[smem, smem] + [pl.BlockSpec(memory_space=pl.ANY)] * group,
        out_specs=pl.BlockSpec(memory_space=pltpu.VMEM),
        scratch_shapes=[pltpu.VMEM(copies[0].shape, bf16), pltpu.SemaphoreType.DMA((group,))],
        compiler_params=params(24),
        name="expand",
    )(codes, distance.reshape(1), *copies)


def layer_body(
    gathered, tails, own, above, above_own, above_scale, weight, here, inv_rms, gain,
    full_out, sent_out, own_out, total, shift,
):
    step, last = pl.program_id(0), pl.num_programs(0) - 1
    width = weight.shape[1]

    @pl.when(step == 0)
    def _():
        dots = jnp.sum(jnp.sum(tails[...].astype(f32), axis=0), axis=1, keepdims=True)
        shift[...] = jnp.broadcast_to(above_scale[...] * dots, shift.shape)
        total[...] = jnp.zeros_like(total)

    factor = shift[:, :1]
    acc = total[...]
    for i in range(gathered.shape[0]):
        piece = gathered[i, :, :width].astype(f32) - factor * above[i].astype(f32)
        piece = piece.astype(bf16)
        full_out[i] = piece
        acc += lax.dot_general(piece, weight[i], across_last, preferred_element_type=f32)
    total[...] = acc

    @pl.when(step == last)
    def _():
        grad = own[...] - factor * above_own[...].astype(f32)
        scaled = gain[...] * acc
        rms = inv_rms[...]
        dots = jnp.sum(scaled * (here[...].astype(f32) * rms), axis=1, keepdims=True)
        result = grad + rms * scaled
        own_out[...] = result
        sent_out[:, :width] = result.astype(bf16)
        high = dots.astype(bf16).astype(f32)
        low = (dots - high).astype(bf16).astype(f32)
        lane = lax.broadcasted_iota(jnp.int32, (dots.shape[0], lanes), 1)
        tail = jnp.where(lane == 0, high, jnp.where(lane == 1, low, 0.0))
        sent_out[:, width:] = tail.astype(bf16)


def layer(gathered, own, above, above_at, above_own, above_scale, weight, here, inv_rms, gain):
    shards, tokens, wide = gathered.shape
    width = wide - lanes
    chunk = min(8, shards)

    def whole(*shape):
        return pl.BlockSpec(shape, lambda c: (0,) * len(shape))

    return pl.pallas_call(
        layer_body,
        grid=(shards // chunk,),
        out_shape=(
            jax.ShapeDtypeStruct((shards, tokens, width), bf16),
            jax.ShapeDtypeStruct((tokens, wide), bf16),
            jax.ShapeDtypeStruct((tokens, width), f32),
        ),
        in_specs=[
            pl.BlockSpec((chunk, tokens, wide), lambda c: (c, 0, 0)),
            pl.BlockSpec((shards, tokens, lanes), lambda c: (0, 0, width // lanes)),
            whole(tokens, width),
            pl.BlockSpec((chunk, tokens, width), lambda c: (c, above_at, 0)),
            whole(tokens, width),
            whole(tokens, 1),
            pl.BlockSpec((chunk, width, width), lambda c: (c, 0, 0)),
            whole(tokens, width),
            whole(tokens, 1),
            whole(1, width),
        ],
        out_specs=(
            pl.BlockSpec((chunk, tokens, width), lambda c: (c, 0, 0)),
            whole(tokens, wide),
            whole(tokens, width),
        ),
        scratch_shapes=[pltpu.VMEM((tokens, width), f32), pltpu.VMEM((tokens, lanes), f32)],
        compiler_params=params(16),
        name="layer",
    )(gathered, gathered, own, above, above_own, above_scale, weight, here, inv_rms, gain)


def grads_body(
    code_ref, came0, came1, came2, came3, inputs, gain, blocks, out, gain_out, right, left, totals,
    *, col_blocks,
):
    size = blocks.shape[1]
    came = (came0, came1, came2, came3)
    shards, part = came0.shape[0] - 1, came0.shape[1]
    for x in range(group):
        rms = jnp.sum(came[x][shards].astype(f32), axis=1, keepdims=True)
        normed = (inputs[x].astype(f32) * rms * gain[...]).astype(bf16)
        right[0, x * part:(x + 1) * part, :] = normed[:, :size]
        right[1, x * part:(x + 1) * part, :] = normed[:, size:]
    for row in range(2):
        left[row] = right[row].astype(f32).T.astype(bf16)
        totals[row] = jnp.zeros_like(totals[row])

    def arrange(shard, carry):
        for x in range(group):
            rows = slice(x * part, (x + 1) * part)
            right[2 * shard, rows, :] = came[x][shard, :, :size]
            right[2 * shard + 1, rows, :] = came[x][shard, :, size:]
        return carry

    lax.fori_loop(0, shards, arrange, 0)
    dead = 2 * col_blocks
    slots = blocks.shape[0]
    several = 4 if slots % 4 == 0 else 2

    def some(first, carry):
        found = []
        for i in range(several):
            code = code_ref[first * several + i]
            live = (code < dead).astype(f32)
            place = code % dead
            row, col = place // col_blocks, place % col_blocks
            grad = jnp.dot(left[row], right[col], preferred_element_type=f32) * live
            found.append((row, grad))
        for i, (row, grad) in enumerate(found):
            slot = first * several + i
            out[slot] = grad.astype(bf16)
            totals[row] += grad * blocks[slot].astype(f32)
        return carry

    lax.fori_loop(0, slots // several, some, 0)
    for row in range(2):
        gain_out[row * size:(row + 1) * size, :] = jnp.sum(totals[row], axis=1, keepdims=True)


def slot_grads(codes, came, inputs, gain, blocks):
    size = blocks.shape[1]
    parts, part, width = inputs.shape
    shards = came[0].shape[0] - 1
    vmem = pl.BlockSpec(memory_space=pltpu.VMEM)
    return pl.pallas_call(
        functools.partial(grads_body, col_blocks=2 * shards),
        out_shape=(
            jax.ShapeDtypeStruct(blocks.shape, bf16),
            jax.ShapeDtypeStruct((width, 1), f32),
        ),
        in_specs=[pl.BlockSpec(memory_space=pltpu.SMEM)] + [vmem] * (group + 3),
        out_specs=(vmem, vmem),
        scratch_shapes=[
            pltpu.VMEM((2 * shards, parts * part, size), bf16),
            pltpu.VMEM((2, size, parts * part), bf16),
            pltpu.VMEM((2, size, size), f32),
        ],
        compiler_params=params(32),
        name="slot_grads",
    )(codes, *came, inputs, gain, blocks)


def in_parts(value):
    parts = []
    for _ in range(3):
        part = lax.reduce_precision(value, 8, 7)
        parts.append(part.astype(bf16))
        value = value - part
    return parts


def per_device(x_saved, gains, w_blocks, slot_pos, slot_live, kl_grads, teacher):
    sections, shards = lax.axis_size("pipe"), lax.axis_size("tp")
    section, shard = lax.axis_index("pipe"), lax.axis_index("tp")
    line, block = section // group, section % group
    lines = sections // group
    together = [[i * group + x for x in range(group)] for i in range(lines)]
    down = [(i, i - group) for i in range(group, sections)]
    tokens, width = x_saved.shape[1], x_saved.shape[2]
    part = tokens // group
    full_width = width * shards
    blocks = w_blocks[0]
    slots = blocks.shape[0]
    places = 4 * shards
    codes = slot_pos[0] - shard * places + places * (1 - slot_live[0])

    code_row = jnp.zeros((width,), f32).at[:slots].set(codes.astype(f32)).astype(bf16)
    notes = jnp.stack(in_parts(gains[0]) + [code_row])
    notes = jnp.concatenate([notes, jnp.zeros((12, width), bf16)])
    notes = jnp.broadcast_to(notes[None], (group,) + notes.shape)
    told = jnp.concatenate([x_saved[0].reshape(group, part, width), notes], axis=1)
    told = lax.all_to_all(told, "pipe", 0, 0, axis_index_groups=together)
    inputs = told[:, :part]
    gain_rows = jnp.sum(told[:, part:part + 3].astype(f32), axis=1)
    line_codes = told[:, part + 3, :slots].astype(jnp.int32)

    def partners(distance, places):
        return [
            (i * group + x, i * group + (x ^ distance)) for i in range(lines) for x in places
        ]

    def spread(array, places):
        return [lax.ppermute(array, "pipe", partners(d, places)) for d in range(1, group)]

    early = spread(blocks, (3, 2))

    first = group - 1
    partial = jnp.sum(jnp.square(inputs[first].astype(f32)), axis=1, keepdims=True)
    entry = jnp.where((teacher == 1)[:, None], kl_grads[1], kl_grads[0])
    entry = lax.dynamic_slice_in_dim(entry, block * part, part, 0)
    own = entry.astype(f32)
    tail = jnp.concatenate(in_parts(partial) + [jnp.zeros((part, lanes - 3), bf16)], axis=1)
    sent = jnp.concatenate([entry, tail], axis=1)
    gathered = lax.all_gather(sent, "tp")
    tails = gathered[:, :, width:].astype(f32)
    first_rms = lax.rsqrt(jnp.sum(tails, axis=(0, 2)) / full_width + norm_epsilon)[:, None]

    all_inputs = lax.all_gather(inputs.reshape(tokens, width), "tp")
    dense = [None] * group
    kept = [None] * group
    for step in range(sections):
        phase, place = step // group, first - step % group
        if phase == 0:
            copies = [blocks] + (early if place >= 2 else late)
            dense[place] = expand(line_codes[place], block ^ place, copies, shards)
        if step == 1:
            gathered = lax.all_gather(sent, "tp")
            gathered, all_inputs = lax.optimization_barrier((gathered, all_inputs))
            squares = jnp.sum(jnp.square(all_inputs.astype(f32)), axis=(0, 2))
            inv_rms = lax.rsqrt(squares / full_width + norm_epsilon).reshape(group, part, 1)
            correct = jnp.square(inv_rms) / full_width
        if step == 0:
            above, above_at, above_own = jnp.zeros_like(gathered[:, :, :width]), 0, inputs[0]
            scale, rms = jnp.zeros((part, 1), f32), first_rms
        elif place == first:
            notes = jnp.concatenate(
                [sent[:, width:width + 2].astype(f32), correct[0]], axis=1
            )
            notes = jnp.pad(notes, ((0, 0), (0, lanes - 3)))
            passed = jnp.concatenate([own, notes, inputs[0].astype(f32)], axis=1)
            passed = lax.ppermute(passed, "pipe", down)
            own = passed[:, :width]
            tail = jnp.pad(passed[:, width:width + 2], ((0, 0), (0, lanes - 2)))
            sent = jnp.concatenate([own, tail], axis=1).astype(bf16)
            scale = passed[:, width + 2:width + 3]
            above, above_at, above_own = upper, 0, passed[:, width + lanes:]
            rms = inv_rms[place]
        else:
            above, above_at = all_inputs, place + 1
            above_own, scale, rms = inputs[place + 1], correct[place + 1], inv_rms[place]
        if step > 1:
            gathered = lax.all_gather(sent, "tp")
        if step == 3:
            gathered, upper = lax.optimization_barrier((gathered, upper))
        full, sent, own = layer(
            gathered, own, above, above_at, above_own, scale, dense[place],
            inputs[place], rms, gain_rows[place][None],
        )
        if step == 0:
            later_blocks, sent = lax.optimization_barrier((blocks, sent))
            late = spread(later_blocks, (1, 0))
        if step == 1:
            upper = lax.ppermute(all_inputs[:, :part], "pipe", down)
        if phase == 0:
            kept[place] = full
        else:
            kept[place] = jnp.where(line == lines - 1 - phase, full, kept[place])

    rms_parts = jnp.concatenate(in_parts(inv_rms), axis=2)
    rms_parts = jnp.pad(rms_parts, ((0, 0), (0, 0), (0, width - 3)))
    leaving = jnp.concatenate([jnp.stack(kept), rms_parts[:, None]], axis=1)
    native = x_saved[0].reshape(group, part, width)
    came, order = [], []
    for distance in range(group):
        other = block ^ distance
        piece = lax.dynamic_index_in_dim(leaving, other, 0, keepdims=False)
        if distance:
            piece = lax.ppermute(piece, "pipe", partners(distance, range(group)))
        came.append(piece)
        order.append(lax.dynamic_index_in_dim(native, other, 0, keepdims=False))
    w_grads, gain_sums = slot_grads(codes, came, jnp.stack(order), gains, blocks)
    return (w_grads[None], gain_sums.reshape(1, width) / gains)


def solution(mesh):
    in_specs = (
        P("pipe", None, "tp"),
        P("pipe", "tp"),
        P("pipe", "tp", None, None),
        P("pipe", "tp"),
        P("pipe", "tp"),
        P(None, None, "tp"),
        P(),
    )
    out_specs = (P("pipe", "tp", None, None), P("pipe", "tp"))
    return jax.shard_map(
        per_device, mesh=mesh, in_specs=in_specs, out_specs=out_specs, check_vma=False
    )
```

```python
import functools

import jax
import jax.numpy as jnp
from jax import lax
from jax.experimental import pallas as pl
from jax.experimental.pallas import tpu as pltpu
from jax.sharding import PartitionSpec as P

norm_epsilon = 1e-05
group = 4
lanes = 128
f32 = jnp.float32
bf16 = jnp.bfloat16
across_last = (((1,), (1,)), ((), ()))


def params(mebibytes):
    return pltpu.CompilerParams(vmem_limit_bytes=mebibytes << 20)


def expand_body(code_ref, came, dense_ref, blocks, arrival, *, place, col_blocks):
    slots, size = blocks.shape[0], blocks.shape[1]
    dead = 2 * col_blocks
    fetch = pltpu.make_async_copy(came.at[place], blocks, arrival)
    fetch.start()
    dense_ref[...] = jnp.zeros_like(dense_ref)
    fetch.wait()

    def put(slot, carry):
        code = code_ref[slot]

        @pl.when(code < dead)
        def _():
            row, col = code // col_blocks, code % col_blocks
            rows = pl.ds(pl.multiple_of(row * size, size), size)
            cols = pl.ds(pl.multiple_of((col % 2) * size, size), size)
            dense_ref[col // 2, rows, cols] = blocks[slot]

        return carry

    lax.fori_loop(0, slots, put, 0)


def expand(codes, weights, place, shards):
    width = 2 * weights.shape[2]
    return pl.pallas_call(
        functools.partial(expand_body, place=place, col_blocks=2 * shards),
        out_shape=jax.ShapeDtypeStruct((shards, width, width), bf16),
        in_specs=[pl.BlockSpec(memory_space=pltpu.SMEM), pl.BlockSpec(memory_space=pl.ANY)],
        out_specs=pl.BlockSpec(memory_space=pltpu.VMEM),
        scratch_shapes=[pltpu.VMEM(weights.shape[1:], bf16), pltpu.SemaphoreType.DMA],
        compiler_params=params(24),
        name="expand",
    )(codes, weights)


def layer_body(
    gathered, tails, own, above, above_own, above_scale, weight, here, inv_rms, gain,
    full_out, sent_out, own_out, total, shift,
):
    step, last = pl.program_id(0), pl.num_programs(0) - 1
    width = weight.shape[1]

    @pl.when(step == 0)
    def _():
        dots = jnp.sum(jnp.sum(tails[...].astype(f32), axis=0), axis=1, keepdims=True)
        shift[...] = jnp.broadcast_to(above_scale[...] * dots, shift.shape)
        total[...] = jnp.zeros_like(total)

    factor = shift[:, :1]
    acc = total[...]
    for i in range(gathered.shape[0]):
        piece = gathered[i, :, :width].astype(f32) - factor * above[i].astype(f32)
        piece = piece.astype(bf16)
        full_out[i] = piece
        acc += lax.dot_general(piece, weight[i], across_last, preferred_element_type=f32)
    total[...] = acc

    @pl.when(step == last)
    def _():
        grad = own[...] - factor * above_own[...].astype(f32)
        scaled = gain[...] * acc
        rms = inv_rms[...]
        dots = jnp.sum(scaled * (here[...].astype(f32) * rms), axis=1, keepdims=True)
        result = grad + rms * scaled
        own_out[...] = result
        sent_out[:, :width] = result.astype(bf16)
        high = dots.astype(bf16).astype(f32)
        low = (dots - high).astype(bf16).astype(f32)
        lane = lax.broadcasted_iota(jnp.int32, (dots.shape[0], lanes), 1)
        tail = jnp.where(lane == 0, high, jnp.where(lane == 1, low, 0.0))
        sent_out[:, width:] = tail.astype(bf16)


def layer(gathered, own, above, above_at, above_own, above_scale, weight, here, inv_rms, gain):
    shards, tokens, wide = gathered.shape
    width = wide - lanes
    chunk = min(8, shards)

    def whole(*shape):
        return pl.BlockSpec(shape, lambda c: (0,) * len(shape))

    return pl.pallas_call(
        layer_body,
        grid=(shards // chunk,),
        out_shape=(
            jax.ShapeDtypeStruct((shards, tokens, width), bf16),
            jax.ShapeDtypeStruct((tokens, wide), bf16),
            jax.ShapeDtypeStruct((tokens, width), f32),
        ),
        in_specs=[
            pl.BlockSpec((chunk, tokens, wide), lambda c: (c, 0, 0)),
            pl.BlockSpec((shards, tokens, lanes), lambda c: (0, 0, width // lanes)),
            whole(tokens, width),
            pl.BlockSpec((chunk, tokens, width), lambda c: (c, above_at, 0)),
            whole(tokens, width),
            whole(tokens, 1),
            pl.BlockSpec((chunk, width, width), lambda c: (c, 0, 0)),
            whole(tokens, width),
            whole(tokens, 1),
            whole(1, width),
        ],
        out_specs=(
            pl.BlockSpec((chunk, tokens, width), lambda c: (c, 0, 0)),
            whole(tokens, wide),
            whole(tokens, width),
        ),
        scratch_shapes=[pltpu.VMEM((tokens, width), f32), pltpu.VMEM((tokens, lanes), f32)],
        compiler_params=params(16),
        name="layer",
    )(gathered, gathered, own, above, above_own, above_scale, weight, here, inv_rms, gain)


def grads_body(
    code_ref, mine, other, inputs, gain, blocks, out, gain_out, right, left, totals,
    *, col_blocks,
):
    size = blocks.shape[1]
    half, part = mine.shape[1] - 1, mine.shape[2]
    slots = blocks.shape[0]
    core = code_ref[slots]
    for x in range(group):
        rms = jnp.sum(mine[x, half].astype(f32), axis=1, keepdims=True)
        normed = (inputs[x].astype(f32) * rms * gain[...]).astype(bf16)
        right[0, x * part:(x + 1) * part, :] = normed[:, :size]
        right[1, x * part:(x + 1) * part, :] = normed[:, size:]
    for row in range(2):
        left[row] = right[row].astype(f32).T.astype(bf16)
        totals[row] = jnp.zeros_like(totals[row])

    def arrange(place, carry):
        for came, base in ((mine, core * half), (other, (1 - core) * half)):
            col = 2 * (base + place)
            for x in range(group):
                rows = slice(x * part, (x + 1) * part)
                right[col, rows, :] = came[x, place, :, :size]
                right[col + 1, rows, :] = came[x, place, :, size:]
        return carry

    lax.fori_loop(0, half, arrange, 0)
    dead = 2 * col_blocks
    several = 4 if slots % 4 == 0 else 2

    def some(first, carry):
        found = []
        for i in range(several):
            code = code_ref[first * several + i]
            live = (code < dead).astype(f32)
            place = code % dead
            row, col = place // col_blocks, place % col_blocks
            grad = jnp.dot(left[row], right[col], preferred_element_type=f32) * live
            found.append((row, grad))
        for i, (row, grad) in enumerate(found):
            slot = first * several + i
            out[slot] = grad.astype(bf16)
            totals[row] += grad * blocks[slot].astype(f32)
        return carry

    lax.fori_loop(0, slots // several, some, 0)
    for row in range(2):
        gain_out[row * size:(row + 1) * size, :] = jnp.sum(totals[row], axis=1, keepdims=True)


def slot_grads(codes, mine, other, inputs, gain, blocks):
    size = blocks.shape[1]
    parts, part, width = inputs.shape
    shards = 2 * (mine.shape[1] - 1)
    vmem = pl.BlockSpec(memory_space=pltpu.VMEM)
    return pl.pallas_call(
        functools.partial(grads_body, col_blocks=2 * shards),
        out_shape=(
            jax.ShapeDtypeStruct(blocks.shape, bf16),
            jax.ShapeDtypeStruct((width, 1), f32),
        ),
        in_specs=[pl.BlockSpec(memory_space=pltpu.SMEM)] + [vmem] * 5,
        out_specs=(vmem, vmem),
        scratch_shapes=[
            pltpu.VMEM((2 * shards, parts * part, size), bf16),
            pltpu.VMEM((2, size, parts * part), bf16),
            pltpu.VMEM((2, size, size), f32),
        ],
        compiler_params=params(32),
        name="slot_grads",
    )(codes, mine, other, inputs, gain, blocks)


def in_parts(value):
    parts = []
    for _ in range(3):
        part = lax.reduce_precision(value, 8, 7)
        parts.append(part.astype(bf16))
        value = value - part
    return parts


def per_device(x_saved, gains, w_blocks, slot_pos, slot_live, kl_grads, teacher):
    sections, shards = lax.axis_size("pipe"), lax.axis_size("tp")
    section, shard = lax.axis_index("pipe"), lax.axis_index("tp")
    line, block = section // group, section % group
    lines = sections // group
    together = [[i * group + x for x in range(group)] for i in range(lines)]
    down = [(i, i - group) for i in range(group, sections)]
    tokens, width = x_saved.shape[1], x_saved.shape[2]
    part = tokens // group
    full_width = width * shards
    blocks = w_blocks[0]
    slots = blocks.shape[0]
    places = 4 * shards
    codes = slot_pos[0] - shard * places + places * (1 - slot_live[0])

    code_row = jnp.zeros((width,), f32).at[:slots].set(codes.astype(f32)).astype(bf16)
    notes = jnp.stack(in_parts(gains[0]) + [code_row])
    notes = jnp.concatenate([notes, jnp.zeros((12, width), bf16)])
    notes = jnp.broadcast_to(notes[None], (group,) + notes.shape)
    told = jnp.concatenate([x_saved[0].reshape(group, part, width), notes], axis=1)
    told = lax.all_to_all(told, "pipe", 0, 0, axis_index_groups=together)
    inputs = told[:, :part]
    gain_rows = jnp.sum(told[:, part:part + 3].astype(f32), axis=1)
    line_codes = told[:, part + 3, :slots].astype(jnp.int32)

    first = group - 1
    weights = lax.all_gather(blocks, "pipe", axis_index_groups=together)
    second_inputs = lax.all_gather(inputs[first], "tp")

    partial = jnp.sum(jnp.square(inputs.astype(f32)), axis=2)
    partial = jnp.concatenate([p.T for p in in_parts(partial)], axis=1)
    partial = jnp.pad(partial, ((0, 0), (0, lanes - 3 * group)))
    entry = jnp.where((teacher == 1)[:, None], kl_grads[1], kl_grads[0])
    entry = lax.dynamic_slice_in_dim(entry, block * part, part, 0)
    own = entry.astype(f32)
    sent = jnp.concatenate([entry, partial], axis=1)
    sent, second_inputs = lax.optimization_barrier((sent, second_inputs))
    gathered = lax.all_gather(sent, "tp")
    squares = jnp.sum(gathered[:, :, width:].astype(f32), axis=0)[:, :3 * group]
    squares = jnp.sum(squares.reshape(part, 3, group), axis=1).T
    inv_rms = lax.rsqrt(squares / full_width + norm_epsilon)[:, :, None]
    correct = jnp.square(inv_rms) / full_width

    third, gathered = lax.optimization_barrier((inputs[first - 1], gathered))
    third_inputs = lax.all_gather(third, "tp")
    weights, third_inputs = lax.optimization_barrier((weights, third_inputs))
    rest, weights = lax.optimization_barrier((inputs[:first - 1], weights))
    rest_inputs = lax.all_gather(rest.reshape((first - 1) * part, width), "tp")

    found = {first: (second_inputs, 0), first - 1: (third_inputs, 0)}
    dense = [None] * group
    kept = [None] * group
    half = shards // 2
    for step in range(sections):
        phase, place = step // group, first - step % group
        if phase == 0:
            dense[place] = expand(line_codes[place], weights, place, shards)
        if step == 0:
            (above, above_at), above_own = found[first], inputs[first]
            scale = jnp.zeros((part, 1), f32)
        elif place == first:
            notes = jnp.concatenate(
                [sent[:, width:width + 2].astype(f32), correct[0]], axis=1
            )
            notes = jnp.pad(notes, ((0, 0), (0, lanes - 3)))
            passed = jnp.concatenate([own, notes, inputs[0].astype(f32)], axis=1)
            passed = lax.ppermute(passed, "pipe", down)
            own = passed[:, :width]
            tail = jnp.pad(passed[:, width:width + 2], ((0, 0), (0, lanes - 2)))
            sent = jnp.concatenate([own, tail], axis=1).astype(bf16)
            scale = passed[:, width + 2:width + 3]
            above, above_at, above_own = upper, 0, passed[:, width + lanes:]
        else:
            (above, above_at), above_own = found[place + 1], inputs[place + 1]
            scale = correct[place + 1]
        if step > 0:
            gathered = lax.all_gather(sent, "tp")
        if step == 2:
            gathered, rest_inputs = lax.optimization_barrier((gathered, rest_inputs))
            found[1], found[0] = (rest_inputs, 1), (rest_inputs, 0)
            upper = lax.ppermute(rest_inputs[:, :part], "pipe", down)
        if step == 3:
            gathered, upper = lax.optimization_barrier((gathered, upper))
        full, sent, own = layer(
            gathered, own, above, above_at, above_own, scale, dense[place],
            inputs[place], inv_rms[place], gain_rows[place][None],
        )
        full = lax.dynamic_slice_in_dim(full, (shard % 2) * half, half, 0)
        if phase == 0:
            kept[place] = full
        else:
            kept[place] = jnp.where(line == lines - 1 - phase, full, kept[place])

    rms_parts = jnp.concatenate(in_parts(inv_rms), axis=2)
    rms_parts = jnp.pad(rms_parts, ((0, 0), (0, 0), (0, width - 3)))
    leaving = jnp.concatenate([jnp.stack(kept), rms_parts[:, None]], axis=1)
    came = lax.all_to_all(leaving, "pipe", 0, 0, axis_index_groups=together)
    other = lax.ppermute(came, "tp", [(i, i ^ 1) for i in range(shards)])
    native = x_saved[0].reshape(group, part, width)
    codes = jnp.concatenate([codes, (shard % 2).astype(jnp.int32)[None]])
    w_grads, gain_sums = slot_grads(codes, came, other, native, gains, blocks)
    return (w_grads[None], gain_sums.reshape(1, width) / gains)


def solution(mesh):
    in_specs = (
        P("pipe", None, "tp"),
        P("pipe", "tp"),
        P("pipe", "tp", None, None),
        P("pipe", "tp"),
        P("pipe", "tp"),
        P(None, None, "tp"),
        P(),
    )
    out_specs = (P("pipe", "tp", None, None), P("pipe", "tp"))
    return jax.shard_map(
        per_device, mesh=mesh, in_specs=in_specs, out_specs=out_specs, check_vma=False
    )
```

```python
import functools

import jax
import jax.numpy as jnp
from jax import lax
from jax.experimental import pallas as pl
from jax.experimental.pallas import tpu as pltpu
from jax.sharding import PartitionSpec as P

norm_epsilon = 1e-05
group = 4
lanes = 128
f32 = jnp.float32
bf16 = jnp.bfloat16
across_last = (((1,), (1,)), ((), ()))


def params(mebibytes):
    return pltpu.CompilerParams(vmem_limit_bytes=mebibytes << 20)


def expand_body(code_ref, came, dense_ref, blocks, arrival, *, place, col_blocks):
    slots, size = blocks.shape[0], blocks.shape[1]
    dead = 2 * col_blocks
    fetch = pltpu.make_async_copy(came.at[place], blocks, arrival)
    fetch.start()
    dense_ref[...] = jnp.zeros_like(dense_ref)
    fetch.wait()

    def put(slot, carry):
        code = code_ref[slot]

        @pl.when(code < dead)
        def _():
            row, col = code // col_blocks, code % col_blocks
            rows = pl.ds(pl.multiple_of(row * size, size), size)
            cols = pl.ds(pl.multiple_of((col % 2) * size, size), size)
            dense_ref[col // 2, rows, cols] = blocks[slot]

        return carry

    lax.fori_loop(0, slots, put, 0)


def expand(codes, weights, place, shards):
    width = 2 * weights.shape[2]
    return pl.pallas_call(
        functools.partial(expand_body, place=place, col_blocks=2 * shards),
        out_shape=jax.ShapeDtypeStruct((shards, width, width), bf16),
        in_specs=[pl.BlockSpec(memory_space=pltpu.SMEM), pl.BlockSpec(memory_space=pltpu.HBM)],
        out_specs=pl.BlockSpec(memory_space=pltpu.VMEM),
        scratch_shapes=[pltpu.VMEM(weights.shape[1:], bf16), pltpu.SemaphoreType.DMA],
        compiler_params=params(24),
        name="expand",
    )(codes, weights)


def layer_body(
    flags, gathered, own, above, above_own, above_scale, weight, here, inv_rms, gain, *rest,
    above_at, told, tell, phase,
):
    rest = list(rest)
    before = None if told else rest.pop(0)
    kept = rest.pop(0) if phase else None
    full_out, sent_out, own_out, kept_out = rest
    shards, width = weight.shape[0], weight.shape[1]
    tokens = own.shape[0]
    rows = slice(above_at * tokens, (above_at + 1) * tokens)

    if told:
        total = gathered[0, :, width:].astype(f32)
        for i in range(1, shards):
            total += gathered[i, :, width:].astype(f32)
    else:
        total = jnp.zeros((tokens, width), f32)
        for i in range(shards):
            change = gathered[i].astype(f32) - before[i].astype(f32)
            total += change * above[i, rows, :].astype(f32)
    factor = above_scale[...] * jnp.sum(total, axis=1, keepdims=True)

    acc = jnp.zeros((tokens, width), f32)
    for i in range(shards):
        piece = gathered[i, :, :width].astype(f32) - factor * above[i, rows, :].astype(f32)
        piece = piece.astype(bf16)
        full_out[i] = piece
        acc += lax.dot_general(piece, weight[i], across_last, preferred_element_type=f32)

    grad = own[...] - factor * above_own[...].astype(f32)
    scaled = gain[...] * acc
    rms = inv_rms[...]
    result = grad + rms * scaled
    own_out[...] = result
    sent_out[:, :width] = result.astype(bf16)
    if tell:
        dots = jnp.sum(scaled * (here[...].astype(f32) * rms), axis=1, keepdims=True)
        high = dots.astype(bf16).astype(f32)
        low = (dots - high).astype(bf16).astype(f32)
        lane = lax.broadcasted_iota(jnp.int32, (tokens, lanes), 1)
        tail = jnp.where(lane == 0, high, jnp.where(lane == 1, low, 0.0))
        sent_out[:, width:] = tail.astype(bf16)

    half = shards // 2
    mine = pl.ds(flags[0] * half, half)
    if phase:

        @pl.when(flags[phase] == 1)
        def _():
            kept_out[...] = full_out[mine]

        @pl.when(flags[phase] == 0)
        def _():
            kept_out[...] = kept[...]
    else:
        kept_out[...] = full_out[mine]


def layer(flags, operands, before, kept, above_at, tell, phase):
    weight, own = operands[5], operands[1]
    shards, width, tokens = weight.shape[0], weight.shape[1], own.shape[0]
    extra = [] if before is None else [before]
    extra += [] if kept is None else [kept]
    vmem = pl.BlockSpec(memory_space=pltpu.VMEM)
    return pl.pallas_call(
        functools.partial(
            layer_body, above_at=above_at, told=before is None, tell=tell, phase=phase
        ),
        out_shape=(
            jax.ShapeDtypeStruct((shards, tokens, width), bf16),
            jax.ShapeDtypeStruct((tokens, width + (lanes if tell else 0)), bf16),
            jax.ShapeDtypeStruct((tokens, width), f32),
            jax.ShapeDtypeStruct((shards // 2, tokens, width), bf16),
        ),
        in_specs=[pl.BlockSpec(memory_space=pltpu.SMEM)] + [vmem] * (len(operands) + len(extra)),
        out_specs=(vmem,) * 4,
        compiler_params=params(16),
        name="layer",
    )(flags, *operands, *extra)


def grads_body(
    code_ref, mine, other, inputs, gain, blocks, out, gain_out, right, left, totals,
    *, col_blocks,
):
    size = blocks.shape[1]
    half, part = mine.shape[1] - 1, mine.shape[2]
    slots = blocks.shape[0]
    core = code_ref[slots]
    for x in range(group):
        rms = jnp.sum(mine[x, half].astype(f32), axis=1, keepdims=True)
        normed = (inputs[x].astype(f32) * rms * gain[...]).astype(bf16)
        right[0, x * part:(x + 1) * part, :] = normed[:, :size]
        right[1, x * part:(x + 1) * part, :] = normed[:, size:]
    for row in range(2):
        left[row] = right[row].astype(f32).T.astype(bf16)
        totals[row] = jnp.zeros_like(totals[row])

    def arrange(place, carry):
        for came, base in ((mine, core * half), (other, (1 - core) * half)):
            col = 2 * (base + place)
            for x in range(group):
                rows = slice(x * part, (x + 1) * part)
                right[col, rows, :] = came[x, place, :, :size]
                right[col + 1, rows, :] = came[x, place, :, size:]
        return carry

    lax.fori_loop(0, half, arrange, 0)
    dead = 2 * col_blocks
    several = 4 if slots % 4 == 0 else 2

    def some(first, carry):
        found = []
        for i in range(several):
            code = code_ref[first * several + i]
            live = (code < dead).astype(f32)
            place = code % dead
            row, col = place // col_blocks, place % col_blocks
            grad = jnp.dot(left[row], right[col], preferred_element_type=f32) * live
            found.append((row, grad))
        for i, (row, grad) in enumerate(found):
            slot = first * several + i
            out[slot] = grad.astype(bf16)
            totals[row] += grad * blocks[slot].astype(f32)
        return carry

    lax.fori_loop(0, slots // several, some, 0)
    for row in range(2):
        gain_out[row * size:(row + 1) * size, :] = jnp.sum(totals[row], axis=1, keepdims=True)


def slot_grads(codes, mine, other, inputs, gain, blocks):
    size = blocks.shape[1]
    parts, part, width = inputs.shape
    shards = 2 * (mine.shape[1] - 1)
    vmem = pl.BlockSpec(memory_space=pltpu.VMEM)
    return pl.pallas_call(
        functools.partial(grads_body, col_blocks=2 * shards),
        out_shape=(
            jax.ShapeDtypeStruct(blocks.shape, bf16),
            jax.ShapeDtypeStruct((width, 1), f32),
        ),
        in_specs=[pl.BlockSpec(memory_space=pltpu.SMEM)] + [vmem] * 5,
        out_specs=(vmem, vmem),
        scratch_shapes=[
            pltpu.VMEM((2 * shards, parts * part, size), bf16),
            pltpu.VMEM((2, size, parts * part), bf16),
            pltpu.VMEM((2, size, size), f32),
        ],
        compiler_params=params(32),
        name="slot_grads",
    )(codes, mine, other, inputs, gain, blocks)


def in_parts(value):
    parts = []
    for _ in range(3):
        part = lax.reduce_precision(value, 8, 7)
        parts.append(part.astype(bf16))
        value = value - part
    return parts


def per_device(x_saved, gains, w_blocks, slot_pos, slot_live, kl_grads, teacher):
    sections, shards = lax.axis_size("pipe"), lax.axis_size("tp")
    section, shard = lax.axis_index("pipe"), lax.axis_index("tp")
    line, block = section // group, section % group
    lines = sections // group
    together = [[i * group + x for x in range(group)] for i in range(lines)]
    down = [(i, i - group) for i in range(group, sections)]
    tokens, width = x_saved.shape[1], x_saved.shape[2]
    part = tokens // group
    full_width = width * shards
    blocks = w_blocks[0]
    slots = blocks.shape[0]
    places = 4 * shards
    codes = slot_pos[0] - shard * places + places * (1 - slot_live[0])

    code_row = jnp.zeros((width,), f32).at[:slots].set(codes.astype(f32)).astype(bf16)
    notes = jnp.stack(in_parts(gains[0]) + [code_row])
    notes = jnp.concatenate([notes, jnp.zeros((12, width), bf16)])
    notes = jnp.broadcast_to(notes[None], (group,) + notes.shape)
    told = jnp.concatenate([x_saved[0].reshape(group, part, width), notes], axis=1)
    told = lax.all_to_all(told, "pipe", 0, 0, axis_index_groups=together)
    inputs = told[:, :part]
    gain_rows = jnp.sum(told[:, part:part + 3].astype(f32), axis=1)
    line_codes = told[:, part + 3, :slots].astype(jnp.int32)

    first = group - 1
    upper_own = lax.ppermute(inputs[0], "pipe", down)
    weights = lax.all_gather(blocks, "pipe", axis_index_groups=together)
    second_inputs = lax.all_gather(inputs[first], "tp")

    partial = jnp.sum(jnp.square(inputs.astype(f32)), axis=2)
    partial = jnp.concatenate([p.T for p in in_parts(partial)], axis=1)
    partial = jnp.pad(partial, ((0, 0), (0, lanes - 3 * group)))
    entry = jnp.where((teacher == 1)[:, None], kl_grads[1], kl_grads[0])
    entry = lax.dynamic_slice_in_dim(entry, block * part, part, 0)
    own = entry.astype(f32)
    sent = jnp.concatenate([entry, partial], axis=1)
    sent, second_inputs = lax.optimization_barrier((sent, second_inputs))
    gathered = lax.all_gather(sent, "tp")
    squares = jnp.sum(gathered[:, :, width:].astype(f32), axis=0)[:, :3 * group]
    squares = jnp.sum(squares.reshape(part, 3, group), axis=1).T
    inv_rms = lax.rsqrt(squares / full_width + norm_epsilon)[:, :, None]
    correct = jnp.square(inv_rms) / full_width

    third, gathered = lax.optimization_barrier((inputs[first - 1], gathered))
    third_inputs = lax.all_gather(third, "tp")
    weights, third_inputs = lax.optimization_barrier((weights, third_inputs))
    rest = jnp.concatenate([inputs[:first - 1].reshape(-1, width), upper_own])
    rest, weights = lax.optimization_barrier((rest, weights))
    rest_inputs = lax.all_gather(rest, "tp")

    found = {first: (second_inputs, 0), first - 1: (third_inputs, 0)}
    flags = [shard % 2] + [line == lines - 1 - phase for phase in range(1, lines)]
    flags = jnp.stack([flag.astype(jnp.int32) for flag in flags])
    dense = [None] * group
    kept = [None] * group
    full = None
    for step in range(sections):
        phase, place = step // group, first - step % group
        if phase == 0:
            dense[place] = expand(line_codes[place], weights, place, shards)
        before = full
        if step == 0:
            (above, above_at), above_own = found[first], inputs[first]
            scale = jnp.zeros((part, 1), f32)
        elif place == first:
            notes = jnp.concatenate(
                [sent[:, width:width + 2].astype(f32), correct[0]], axis=1
            )
            notes = jnp.pad(notes, ((0, 0), (0, lanes - 3)))
            passed = jnp.concatenate([own, notes], axis=1)
            passed = lax.ppermute(passed, "pipe", down)
            own = passed[:, :width]
            tail = jnp.pad(passed[:, width:width + 2], ((0, 0), (0, lanes - 2)))
            sent = jnp.concatenate([own, tail], axis=1).astype(bf16)
            scale = passed[:, width + 2:width + 3]
            above, above_at, above_own = rest_inputs, 2, upper_own
            before = None
        else:
            (above, above_at), above_own = found[place + 1], inputs[place + 1]
            scale = correct[place + 1]
        if step > 0:
            gathered = lax.all_gather(sent, "tp")
        if step == 2:
            gathered, rest_inputs = lax.optimization_barrier((gathered, rest_inputs))
            found[1], found[0] = (rest_inputs, 1), (rest_inputs, 0)
        operands = (
            gathered, own, above, above_own, scale, dense[place],
            inputs[place], inv_rms[place], gain_rows[place][None],
        )
        tell = place == 0 and step < sections - 1
        full, sent, own, kept[place] = layer(
            flags, operands, before, kept[place], above_at, tell, phase
        )

    rms_parts = jnp.concatenate(in_parts(inv_rms), axis=2)
    rms_parts = jnp.pad(rms_parts, ((0, 0), (0, 0), (0, width - 3)))
    leaving = jnp.concatenate([jnp.stack(kept), rms_parts[:, None]], axis=1)
    came = lax.all_to_all(leaving, "pipe", 0, 0, axis_index_groups=together)
    other = lax.ppermute(came, "tp", [(i, i ^ 1) for i in range(shards)])
    native = x_saved[0].reshape(group, part, width)
    codes = jnp.concatenate([codes, (shard % 2).astype(jnp.int32)[None]])
    w_grads, gain_sums = slot_grads(codes, came, other, native, gains, blocks)
    return (w_grads[None], gain_sums.reshape(1, width) / gains)


def solution(mesh):
    in_specs = (
        P("pipe", None, "tp"),
        P("pipe", "tp"),
        P("pipe", "tp", None, None),
        P("pipe", "tp"),
        P("pipe", "tp"),
        P(None, None, "tp"),
        P(),
    )
    out_specs = (P("pipe", "tp", None, None), P("pipe", "tp"))
    return jax.shard_map(
        per_device, mesh=mesh, in_specs=in_specs, out_specs=out_specs, check_vma=False
    )
```

```python
import functools

import jax
import jax.numpy as jnp
from jax import lax
from jax.experimental import pallas as pl
from jax.experimental.pallas import tpu as pltpu
from jax.sharding import PartitionSpec as P

norm_epsilon = 1e-05
group = 4
lanes = 128
f32 = jnp.float32
bf16 = jnp.bfloat16
across_last = (((1,), (1,)), ((), ()))


def params(mebibytes):
    return pltpu.CompilerParams(vmem_limit_bytes=mebibytes << 20)


def block_of(code, col_blocks):
    row = lax.shift_right_logical(code, col_blocks.bit_length() - 1) & 1
    return row, code & (col_blocks - 1)


def at_once(slots, most):
    return max(n for n in range(1, most + 1) if slots % n == 0)


def expand_body(code_ref, came, *dense, col_blocks):
    slots, size = came.shape[1], came.shape[2]
    several = at_once(slots, 8)
    for place in reversed(range(group)):
        rows_of = dense[place]
        rows_of[...] = jnp.zeros_like(rows_of)

        def some(first, carry):
            for i in range(several):
                slot = first * several + i
                code = code_ref[place * slots + slot]
                row, col = block_of(code, col_blocks)
                rows = pl.ds(pl.multiple_of(row * size, size), size)
                cols = pl.ds(pl.multiple_of((col & 1) * size, size), size)
                block = came[place, slot]
                block = jnp.where(code < 2 * col_blocks, block, jnp.zeros_like(block))
                rows_of[lax.shift_right_logical(col, 1), rows, cols] = block
            return carry

        lax.fori_loop(0, slots // several, some, 0)


def expand(codes, weights, shards):
    width = 2 * weights.shape[2]
    vmem = pl.BlockSpec(memory_space=pltpu.VMEM)
    return pl.pallas_call(
        functools.partial(expand_body, col_blocks=2 * shards),
        out_shape=(jax.ShapeDtypeStruct((shards, width, width), bf16),) * group,
        in_specs=[pl.BlockSpec(memory_space=pltpu.SMEM), vmem],
        out_specs=(vmem,) * group,
        compiler_params=params(32),
        name="expand",
    )(codes.reshape(-1), weights)


def layer_body(
    flags, gathered, own, above, above_own, above_scale, weight, here, inv_rms, gain, *rest,
    above_at, told, tell, phase,
):
    rest = list(rest)
    before = None if told else rest.pop(0)
    kept = rest.pop(0) if phase else None
    full_out, sent_out, own_out, kept_out = rest
    shards, width = weight.shape[0], weight.shape[1]
    tokens = own.shape[0]
    rows = slice(above_at * tokens, (above_at + 1) * tokens)

    if told:
        total = gathered[0, :, width:].astype(f32)
        for i in range(1, shards):
            total += gathered[i, :, width:].astype(f32)
    else:
        total = jnp.zeros((tokens, width), f32)
        for i in range(shards):
            change = gathered[i].astype(f32) - before[i].astype(f32)
            total += change * above[i, rows, :].astype(f32)
    factor = above_scale[...] * jnp.sum(total, axis=1, keepdims=True)

    acc = jnp.zeros((tokens, width), f32)
    for i in range(shards):
        piece = gathered[i, :, :width].astype(f32) - factor * above[i, rows, :].astype(f32)
        piece = piece.astype(bf16)
        full_out[i] = piece
        acc += lax.dot_general(piece, weight[i], across_last, preferred_element_type=f32)

    grad = own[...] - factor * above_own[...].astype(f32)
    scaled = gain[...] * acc
    rms = inv_rms[...]
    result = grad + rms * scaled
    own_out[...] = result
    sent_out[:, :width] = result.astype(bf16)
    if tell:
        dots = jnp.sum(scaled * (here[...].astype(f32) * rms), axis=1, keepdims=True)
        high = dots.astype(bf16).astype(f32)
        low = (dots - high).astype(bf16).astype(f32)
        lane = lax.broadcasted_iota(jnp.int32, (tokens, lanes), 1)
        tail = jnp.where(lane == 0, high, jnp.where(lane == 1, low, 0.0))
        sent_out[:, width:] = tail.astype(bf16)

    half = shards // 2
    mine = pl.ds(flags[0] * half, half)
    if phase:

        @pl.when(flags[phase] == 1)
        def _():
            kept_out[...] = full_out[mine]

        @pl.when(flags[phase] == 0)
        def _():
            kept_out[...] = kept[...]
    else:
        kept_out[...] = full_out[mine]


def layer(flags, operands, before, kept, above_at, tell, phase):
    weight, own = operands[5], operands[1]
    shards, width, tokens = weight.shape[0], weight.shape[1], own.shape[0]
    extra = [] if before is None else [before]
    extra += [] if kept is None else [kept]
    vmem = pl.BlockSpec(memory_space=pltpu.VMEM)
    return pl.pallas_call(
        functools.partial(
            layer_body, above_at=above_at, told=before is None, tell=tell, phase=phase
        ),
        out_shape=(
            jax.ShapeDtypeStruct((shards, tokens, width), bf16),
            jax.ShapeDtypeStruct((tokens, width + (lanes if tell else 0)), bf16),
            jax.ShapeDtypeStruct((tokens, width), f32),
            jax.ShapeDtypeStruct((shards // 2, tokens, width), bf16),
        ),
        in_specs=[pl.BlockSpec(memory_space=pltpu.SMEM)] + [vmem] * (len(operands) + len(extra)),
        out_specs=(vmem,) * 4,
        compiler_params=params(12),
        name="layer",
    )(flags, *operands, *extra)


def grads_body(
    code_ref, mine, other, inputs, gain, blocks, out, gain_out, right, left, totals,
    *, col_blocks,
):
    size = blocks.shape[1]
    half, part = mine.shape[1] - 1, mine.shape[2]
    slots = blocks.shape[0]
    core = code_ref[slots]
    for x in range(group):
        rms = jnp.sum(mine[x, half].astype(f32), axis=1, keepdims=True)
        normed = (inputs[x].astype(f32) * rms * gain[...]).astype(bf16)
        right[0, x * part:(x + 1) * part, :] = normed[:, :size]
        right[1, x * part:(x + 1) * part, :] = normed[:, size:]
    for row in range(2):
        left[row] = right[row].astype(f32).T.astype(bf16)
        totals[row] = jnp.zeros_like(totals[row])

    def arrange(place, carry):
        for came, base in ((mine, core * half), (other, (1 - core) * half)):
            col = 2 * (base + place)
            for x in range(group):
                rows = slice(x * part, (x + 1) * part)
                right[col, rows, :] = came[x, place, :, :size]
                right[col + 1, rows, :] = came[x, place, :, size:]
        return carry

    lax.fori_loop(0, half, arrange, 0)
    dead = 2 * col_blocks
    several = at_once(slots, 4)

    def some(first, carry):
        found = []
        for i in range(several):
            code = code_ref[first * several + i]
            live = (code < dead).astype(f32)
            row, col = block_of(code, col_blocks)
            grad = jnp.dot(left[row], right[col], preferred_element_type=f32) * live
            found.append((row, grad))
        for i, (row, grad) in enumerate(found):
            slot = first * several + i
            out[slot] = grad.astype(bf16)
            totals[row] += grad * blocks[slot].astype(f32)
        return carry

    lax.fori_loop(0, slots // several, some, 0)
    for row in range(2):
        gain_out[row * size:(row + 1) * size, :] = jnp.sum(totals[row], axis=1, keepdims=True)


def slot_grads(codes, mine, other, inputs, gain, blocks):
    size = blocks.shape[1]
    parts, part, width = inputs.shape
    shards = 2 * (mine.shape[1] - 1)
    vmem = pl.BlockSpec(memory_space=pltpu.VMEM)
    return pl.pallas_call(
        functools.partial(grads_body, col_blocks=2 * shards),
        out_shape=(
            jax.ShapeDtypeStruct(blocks.shape, bf16),
            jax.ShapeDtypeStruct((width, 1), f32),
        ),
        in_specs=[pl.BlockSpec(memory_space=pltpu.SMEM)] + [vmem] * 5,
        out_specs=(vmem, vmem),
        scratch_shapes=[
            pltpu.VMEM((2 * shards, parts * part, size), bf16),
            pltpu.VMEM((2, size, parts * part), bf16),
            pltpu.VMEM((2, size, size), f32),
        ],
        compiler_params=params(20),
        name="slot_grads",
    )(codes, mine, other, inputs, gain, blocks)


def in_parts(value):
    parts = []
    for _ in range(3):
        part = lax.reduce_precision(value, 8, 7)
        parts.append(part.astype(bf16))
        value = value - part
    return parts


def per_device(x_saved, gains, w_blocks, slot_pos, slot_live, kl_grads, teacher):
    sections, shards = lax.axis_size("pipe"), lax.axis_size("tp")
    section, shard = lax.axis_index("pipe"), lax.axis_index("tp")
    line, block = section // group, section % group
    lines = sections // group
    together = [[i * group + x for x in range(group)] for i in range(lines)]
    down = [(i, i - group) for i in range(group, sections)]
    tokens, width = x_saved.shape[1], x_saved.shape[2]
    part = tokens // group
    full_width = width * shards
    blocks = w_blocks[0]
    slots = blocks.shape[0]
    places = 4 * shards
    codes = slot_pos[0] - shard * places + places * (1 - slot_live[0])

    code_row = jnp.zeros((width,), f32).at[:slots].set(codes.astype(f32)).astype(bf16)
    notes = jnp.stack(in_parts(gains[0]) + [code_row])
    notes = jnp.concatenate([notes, jnp.zeros((12, width), bf16)])
    notes = jnp.broadcast_to(notes[None], (group,) + notes.shape)
    told = jnp.concatenate([x_saved[0].reshape(group, part, width), notes], axis=1)
    told = lax.all_to_all(told, "pipe", 0, 0, axis_index_groups=together)
    inputs = told[:, :part]
    gain_rows = jnp.sum(told[:, part:part + 3].astype(f32), axis=1)
    line_codes = told[:, part + 3, :slots].astype(jnp.int32)

    first = group - 1
    upper_own = lax.ppermute(inputs[0], "pipe", down)
    weights = lax.all_gather(blocks, "pipe", axis_index_groups=together)
    second_inputs = lax.all_gather(inputs[first], "tp")

    partial = jnp.sum(jnp.square(inputs.astype(f32)), axis=2)
    partial = jnp.concatenate([p.T for p in in_parts(partial)], axis=1)
    partial = jnp.pad(partial, ((0, 0), (0, lanes - 3 * group)))
    entry = jnp.where((teacher == 1)[:, None], kl_grads[1], kl_grads[0])
    entry = lax.dynamic_slice_in_dim(entry, block * part, part, 0)
    own = entry.astype(f32)
    sent = jnp.concatenate([entry, partial], axis=1)
    sent, second_inputs = lax.optimization_barrier((sent, second_inputs))
    gathered = lax.all_gather(sent, "tp")
    squares = jnp.sum(gathered[:, :, width:].astype(f32), axis=0)[:, :3 * group]
    squares = jnp.sum(squares.reshape(part, 3, group), axis=1).T
    inv_rms = lax.rsqrt(squares / full_width + norm_epsilon)[:, :, None]
    correct = jnp.square(inv_rms) / full_width

    third, gathered = lax.optimization_barrier((inputs[first - 1], gathered))
    third_inputs = lax.all_gather(third, "tp")
    weights, third_inputs = lax.optimization_barrier((weights, third_inputs))
    rest = jnp.concatenate([inputs[:first - 1].reshape(-1, width), upper_own])
    rest, weights = lax.optimization_barrier((rest, weights))
    rest_inputs = lax.all_gather(rest, "tp")

    found = {first: (second_inputs, 0), first - 1: (third_inputs, 0)}
    flags = [shard % 2] + [line == lines - 1 - phase for phase in range(1, lines)]
    flags = jnp.stack([flag.astype(jnp.int32) for flag in flags])
    dense = expand(line_codes, weights, shards)
    kept = [None] * group
    full = None
    for step in range(sections):
        phase, place = step // group, first - step % group
        before = full
        if step == 0:
            (above, above_at), above_own = found[first], inputs[first]
            scale = jnp.zeros((part, 1), f32)
        elif place == first:
            notes = jnp.concatenate(
                [sent[:, width:width + 2].astype(f32), correct[0]], axis=1
            )
            notes = jnp.pad(notes, ((0, 0), (0, lanes - 3)))
            passed = jnp.concatenate([own, notes], axis=1)
            passed = lax.ppermute(passed, "pipe", down)
            own = passed[:, :width]
            tail = jnp.pad(passed[:, width:width + 2], ((0, 0), (0, lanes - 2)))
            sent = jnp.concatenate([own, tail], axis=1).astype(bf16)
            scale = passed[:, width + 2:width + 3]
            above, above_at, above_own = rest_inputs, 2, upper_own
            before = None
        else:
            (above, above_at), above_own = found[place + 1], inputs[place + 1]
            scale = correct[place + 1]
        if step > 0:
            gathered = lax.all_gather(sent, "tp")
        if step == 2:
            gathered, rest_inputs = lax.optimization_barrier((gathered, rest_inputs))
            found[1], found[0] = (rest_inputs, 1), (rest_inputs, 0)
        operands = (
            gathered, own, above, above_own, scale, dense[place],
            inputs[place], inv_rms[place], gain_rows[place][None],
        )
        tell = place == 0 and step < sections - 1
        full, sent, own, kept[place] = layer(
            flags, operands, before, kept[place], above_at, tell, phase
        )

    rms_parts = jnp.concatenate(in_parts(inv_rms), axis=2)
    rms_parts = jnp.pad(rms_parts, ((0, 0), (0, 0), (0, width - 3)))
    leaving = jnp.concatenate([jnp.stack(kept), rms_parts[:, None]], axis=1)
    came = lax.all_to_all(leaving, "pipe", 0, 0, axis_index_groups=together)
    other = lax.ppermute(came, "tp", [(i, i ^ 1) for i in range(shards)])
    native = x_saved[0].reshape(group, part, width)
    codes = jnp.concatenate([codes, (shard % 2).astype(jnp.int32)[None]])
    w_grads, gain_sums = slot_grads(codes, came, other, native, gains, blocks)
    return (w_grads[None], gain_sums.reshape(1, width) / gains)


def solution(mesh):
    in_specs = (
        P("pipe", None, "tp"),
        P("pipe", "tp"),
        P("pipe", "tp", None, None),
        P("pipe", "tp"),
        P("pipe", "tp"),
        P(None, None, "tp"),
        P(),
    )
    out_specs = (P("pipe", "tp", None, None), P("pipe", "tp"))
    return jax.shard_map(
        per_device, mesh=mesh, in_specs=in_specs, out_specs=out_specs, check_vma=False
    )
```

```python
import functools

import jax
import jax.numpy as jnp
from jax import lax
from jax.experimental import pallas as pl
from jax.experimental.pallas import tpu as pltpu
from jax.sharding import PartitionSpec as P

norm_epsilon = 1e-05
group = 4
lanes = 128
f32 = jnp.float32
bf16 = jnp.bfloat16
across_last = (((1,), (1,)), ((), ()))


def params(mebibytes):
    return pltpu.CompilerParams(vmem_limit_bytes=mebibytes << 20)


def block_of(code, col_blocks):
    row = lax.shift_right_logical(code, col_blocks.bit_length() - 1) & 1
    return row, code & (col_blocks - 1)


def at_once(slots, most):
    return max(n for n in range(1, most + 1) if slots % n == 0)


def expand_body(code_ref, came, *rest, col_blocks):
    dense, (blocks, filled, arrival, leaving) = rest[:group], rest[group:]
    slots, size = came.shape[1], came.shape[2]
    several = at_once(slots, 8)
    order = list(reversed(range(group)))
    fetches = [
        pltpu.make_async_copy(came.at[place], blocks.at[place], arrival.at[place])
        for place in order
    ]
    stores = [
        pltpu.make_async_copy(filled.at[i % 2], dense[place], leaving.at[place])
        for i, place in enumerate(order)
    ]
    for fetch in fetches:
        fetch.start()
    for i, place in enumerate(order):
        if i >= 2:
            stores[i - 2].wait()
        rows_of = filled.at[i % 2]
        rows_of[...] = jnp.zeros_like(rows_of)
        fetches[i].wait()

        def some(first, carry):
            for j in range(several):
                slot = first * several + j
                code = code_ref[place * slots + slot]
                row, col = block_of(code, col_blocks)
                rows = pl.ds(pl.multiple_of(row * size, size), size)
                cols = pl.ds(pl.multiple_of((col & 1) * size, size), size)
                block = blocks[place, slot]
                block = jnp.where(code < 2 * col_blocks, block, jnp.zeros_like(block))
                rows_of[lax.shift_right_logical(col, 1), rows, cols] = block
            return carry

        lax.fori_loop(0, slots // several, some, 0)
        stores[i].start()
    for store in stores[-2:]:
        store.wait()


def expand(codes, weights, shards):
    width = 2 * weights.shape[2]
    hbm = pl.BlockSpec(memory_space=pltpu.HBM)
    return pl.pallas_call(
        functools.partial(expand_body, col_blocks=2 * shards),
        out_shape=(jax.ShapeDtypeStruct((shards, width, width), bf16),) * group,
        in_specs=[pl.BlockSpec(memory_space=pltpu.SMEM), hbm],
        out_specs=(hbm,) * group,
        scratch_shapes=[
            pltpu.VMEM(weights.shape, bf16),
            pltpu.VMEM((2, shards, width, width), bf16),
            pltpu.SemaphoreType.DMA((group,)),
            pltpu.SemaphoreType.DMA((group,)),
        ],
        compiler_params=params(44),
        name="expand",
    )(codes.reshape(-1), weights)


def layer_body(
    flags, gathered, own, above, above_own, above_scale, weight, here, inv_rms, gain, *rest,
    above_at, told, tell, phase,
):
    rest = list(rest)
    before = None if told else rest.pop(0)
    kept = rest.pop(0) if phase else None
    full_out, sent_out, own_out, kept_out = rest
    shards, width = weight.shape[0], weight.shape[1]
    tokens = own.shape[0]
    rows = slice(above_at * tokens, (above_at + 1) * tokens)

    if told:
        total = gathered[0, :, width:].astype(f32)
        for i in range(1, shards):
            total += gathered[i, :, width:].astype(f32)
    else:
        total = jnp.zeros((tokens, width), f32)
        for i in range(shards):
            change = gathered[i].astype(f32) - before[i].astype(f32)
            total += change * above[i, rows, :].astype(f32)
    factor = above_scale[...] * jnp.sum(total, axis=1, keepdims=True)

    acc = jnp.zeros((tokens, width), f32)
    for i in range(shards):
        piece = gathered[i, :, :width].astype(f32) - factor * above[i, rows, :].astype(f32)
        piece = piece.astype(bf16)
        full_out[i] = piece
        acc += lax.dot_general(piece, weight[i], across_last, preferred_element_type=f32)

    grad = own[...] - factor * above_own[...].astype(f32)
    scaled = gain[...] * acc
    rms = inv_rms[...]
    result = grad + rms * scaled
    own_out[...] = result
    sent_out[:, :width] = result.astype(bf16)
    if tell:
        dots = jnp.sum(scaled * (here[...].astype(f32) * rms), axis=1, keepdims=True)
        high = dots.astype(bf16).astype(f32)
        low = (dots - high).astype(bf16).astype(f32)
        lane = lax.broadcasted_iota(jnp.int32, (tokens, lanes), 1)
        tail = jnp.where(lane == 0, high, jnp.where(lane == 1, low, 0.0))
        sent_out[:, width:] = tail.astype(bf16)

    half = shards // 2
    mine = pl.ds(flags[0] * half, half)
    if phase:

        @pl.when(flags[phase] == 1)
        def _():
            kept_out[...] = full_out[mine]

        @pl.when(flags[phase] == 0)
        def _():
            kept_out[...] = kept[...]
    else:
        kept_out[...] = full_out[mine]


def layer(flags, operands, before, kept, above_at, tell, phase):
    weight, own = operands[5], operands[1]
    shards, width, tokens = weight.shape[0], weight.shape[1], own.shape[0]
    extra = [] if before is None else [before]
    extra += [] if kept is None else [kept]
    vmem = pl.BlockSpec(memory_space=pltpu.VMEM)
    return pl.pallas_call(
        functools.partial(
            layer_body, above_at=above_at, told=before is None, tell=tell, phase=phase
        ),
        out_shape=(
            jax.ShapeDtypeStruct((shards, tokens, width), bf16),
            jax.ShapeDtypeStruct((tokens, width + (lanes if tell else 0)), bf16),
            jax.ShapeDtypeStruct((tokens, width), f32),
            jax.ShapeDtypeStruct((shards // 2, tokens, width), bf16),
        ),
        in_specs=[pl.BlockSpec(memory_space=pltpu.SMEM)] + [vmem] * (len(operands) + len(extra)),
        out_specs=(vmem,) * 4,
        compiler_params=params(12),
        name="layer",
    )(flags, *operands, *extra)


def grads_body(
    code_ref, mine, other, inputs, gain, blocks, out, gain_out, right, left, totals,
    *, col_blocks,
):
    size = blocks.shape[1]
    half, part = mine.shape[1] - 1, mine.shape[2]
    slots = blocks.shape[0]
    core = code_ref[slots]
    for x in range(group):
        rms = jnp.sum(mine[x, half].astype(f32), axis=1, keepdims=True)
        normed = (inputs[x].astype(f32) * rms * gain[...]).astype(bf16)
        right[0, x * part:(x + 1) * part, :] = normed[:, :size]
        right[1, x * part:(x + 1) * part, :] = normed[:, size:]
    for row in range(2):
        left[row] = right[row].astype(f32).T.astype(bf16)
        totals[row] = jnp.zeros_like(totals[row])

    def arrange(place, carry):
        for came, base in ((mine, core * half), (other, (1 - core) * half)):
            col = 2 * (base + place)
            for x in range(group):
                rows = slice(x * part, (x + 1) * part)
                right[col, rows, :] = came[x, place, :, :size]
                right[col + 1, rows, :] = came[x, place, :, size:]
        return carry

    lax.fori_loop(0, half, arrange, 0)
    dead = 2 * col_blocks
    several = at_once(slots, 4)

    def some(first, carry):
        found = []
        for i in range(several):
            code = code_ref[first * several + i]
            live = (code < dead).astype(f32)
            row, col = block_of(code, col_blocks)
            grad = jnp.dot(left[row], right[col], preferred_element_type=f32) * live
            found.append((row, grad))
        for i, (row, grad) in enumerate(found):
            slot = first * several + i
            out[slot] = grad.astype(bf16)
            totals[row] += grad * blocks[slot].astype(f32)
        return carry

    lax.fori_loop(0, slots // several, some, 0)
    for row in range(2):
        gain_out[row * size:(row + 1) * size, :] = jnp.sum(totals[row], axis=1, keepdims=True)


def slot_grads(codes, mine, other, inputs, gain, blocks):
    size = blocks.shape[1]
    parts, part, width = inputs.shape
    shards = 2 * (mine.shape[1] - 1)
    vmem = pl.BlockSpec(memory_space=pltpu.VMEM)
    return pl.pallas_call(
        functools.partial(grads_body, col_blocks=2 * shards),
        out_shape=(
            jax.ShapeDtypeStruct(blocks.shape, bf16),
            jax.ShapeDtypeStruct((width, 1), f32),
        ),
        in_specs=[pl.BlockSpec(memory_space=pltpu.SMEM)] + [vmem] * 5,
        out_specs=(vmem, vmem),
        scratch_shapes=[
            pltpu.VMEM((2 * shards, parts * part, size), bf16),
            pltpu.VMEM((2, size, parts * part), bf16),
            pltpu.VMEM((2, size, size), f32),
        ],
        compiler_params=params(32),
        name="slot_grads",
    )(codes, mine, other, inputs, gain, blocks)


def in_parts(value):
    parts = []
    for _ in range(3):
        part = lax.reduce_precision(value, 8, 7)
        parts.append(part.astype(bf16))
        value = value - part
    return parts


def per_device(x_saved, gains, w_blocks, slot_pos, slot_live, kl_grads, teacher):
    sections, shards = lax.axis_size("pipe"), lax.axis_size("tp")
    section, shard = lax.axis_index("pipe"), lax.axis_index("tp")
    line, block = section // group, section % group
    lines = sections // group
    together = [[i * group + x for x in range(group)] for i in range(lines)]
    down = [(i, i - group) for i in range(group, sections)]
    tokens, width = x_saved.shape[1], x_saved.shape[2]
    part = tokens // group
    full_width = width * shards
    blocks = w_blocks[0]
    slots = blocks.shape[0]
    places = 4 * shards
    codes = slot_pos[0] - shard * places + places * (1 - slot_live[0])

    code_row = jnp.zeros((width,), f32).at[:slots].set(codes.astype(f32)).astype(bf16)
    notes = jnp.stack(in_parts(gains[0]) + [code_row])
    notes = jnp.concatenate([notes, jnp.zeros((12, width), bf16)])
    notes = jnp.broadcast_to(notes[None], (group,) + notes.shape)
    told = jnp.concatenate([x_saved[0].reshape(group, part, width), notes], axis=1)
    told = lax.all_to_all(told, "pipe", 0, 0, axis_index_groups=together)
    inputs = told[:, :part]
    gain_rows = jnp.sum(told[:, part:part + 3].astype(f32), axis=1)
    line_codes = told[:, part + 3, :slots].astype(jnp.int32)

    first = group - 1
    upper_own = lax.ppermute(inputs[0], "pipe", down)
    weights = lax.all_gather(blocks, "pipe", axis_index_groups=together)
    second_inputs = lax.all_gather(inputs[first], "tp")

    partial = jnp.sum(jnp.square(inputs.astype(f32)), axis=2)
    partial = jnp.concatenate([p.T for p in in_parts(partial)], axis=1)
    partial = jnp.pad(partial, ((0, 0), (0, lanes - 3 * group)))
    entry = jnp.where((teacher == 1)[:, None], kl_grads[1], kl_grads[0])
    entry = lax.dynamic_slice_in_dim(entry, block * part, part, 0)
    own = entry.astype(f32)
    sent = jnp.concatenate([entry, partial], axis=1)
    sent, second_inputs = lax.optimization_barrier((sent, second_inputs))
    gathered = lax.all_gather(sent, "tp")
    squares = jnp.sum(gathered[:, :, width:].astype(f32), axis=0)[:, :3 * group]
    squares = jnp.sum(squares.reshape(part, 3, group), axis=1).T
    inv_rms = lax.rsqrt(squares / full_width + norm_epsilon)[:, :, None]
    correct = jnp.square(inv_rms) / full_width

    third, gathered = lax.optimization_barrier((inputs[first - 1], gathered))
    third_inputs = lax.all_gather(third, "tp")
    weights, third_inputs = lax.optimization_barrier((weights, third_inputs))
    rest = jnp.concatenate([inputs[:first - 1].reshape(-1, width), upper_own])
    rest, weights = lax.optimization_barrier((rest, weights))
    rest_inputs = lax.all_gather(rest, "tp")

    found = {first: (second_inputs, 0), first - 1: (third_inputs, 0)}
    flags = [shard % 2] + [line == lines - 1 - phase for phase in range(1, lines)]
    flags = jnp.stack([flag.astype(jnp.int32) for flag in flags])
    dense = expand(line_codes, weights, shards)
    kept = [None] * group
    full = None
    for step in range(sections):
        phase, place = step // group, first - step % group
        before = full
        if step == 0:
            (above, above_at), above_own = found[first], inputs[first]
            scale = jnp.zeros((part, 1), f32)
        elif place == first:
            notes = jnp.concatenate(
                [sent[:, width:width + 2].astype(f32), correct[0]], axis=1
            )
            notes = jnp.pad(notes, ((0, 0), (0, lanes - 3)))
            passed = jnp.concatenate([own, notes], axis=1)
            passed = lax.ppermute(passed, "pipe", down)
            own = passed[:, :width]
            tail = jnp.pad(passed[:, width:width + 2], ((0, 0), (0, lanes - 2)))
            sent = jnp.concatenate([own, tail], axis=1).astype(bf16)
            scale = passed[:, width + 2:width + 3]
            above, above_at, above_own = rest_inputs, 2, upper_own
            before = None
        else:
            (above, above_at), above_own = found[place + 1], inputs[place + 1]
            scale = correct[place + 1]
        if step > 0:
            gathered = lax.all_gather(sent, "tp")
        if step == 2:
            gathered, rest_inputs = lax.optimization_barrier((gathered, rest_inputs))
            found[1], found[0] = (rest_inputs, 1), (rest_inputs, 0)
        operands = (
            gathered, own, above, above_own, scale, dense[place],
            inputs[place], inv_rms[place], gain_rows[place][None],
        )
        tell = place == 0 and step < sections - 1
        full, sent, own, kept[place] = layer(
            flags, operands, before, kept[place], above_at, tell, phase
        )

    rms_parts = jnp.concatenate(in_parts(inv_rms), axis=2)
    rms_parts = jnp.pad(rms_parts, ((0, 0), (0, 0), (0, width - 3)))
    leaving = jnp.concatenate([jnp.stack(kept), rms_parts[:, None]], axis=1)
    came = lax.all_to_all(leaving, "pipe", 0, 0, axis_index_groups=together)
    other = lax.ppermute(came, "tp", [(i, i ^ 1) for i in range(shards)])
    native = x_saved[0].reshape(group, part, width)
    codes = jnp.concatenate([codes, (shard % 2).astype(jnp.int32)[None]])
    w_grads, gain_sums = slot_grads(codes, came, other, native, gains, blocks)
    return (w_grads[None], gain_sums.reshape(1, width) / gains)


def solution(mesh):
    in_specs = (
        P("pipe", None, "tp"),
        P("pipe", "tp"),
        P("pipe", "tp", None, None),
        P("pipe", "tp"),
        P("pipe", "tp"),
        P(None, None, "tp"),
        P(),
    )
    out_specs = (P("pipe", "tp", None, None), P("pipe", "tp"))
    return jax.shard_map(
        per_device, mesh=mesh, in_specs=in_specs, out_specs=out_specs, check_vma=False
    )
```

```python
import functools

import jax
import jax.numpy as jnp
from jax import lax
from jax.experimental import pallas as pl
from jax.experimental.pallas import tpu as pltpu
from jax.sharding import PartitionSpec as P

norm_epsilon = 1e-05
group = 4
lanes = 128
f32 = jnp.float32
bf16 = jnp.bfloat16
across_last = (((1,), (1,)), ((), ()))


def params(mebibytes):
    return pltpu.CompilerParams(vmem_limit_bytes=mebibytes << 20)


def block_of(code, col_blocks):
    row = lax.shift_right_logical(code, col_blocks.bit_length() - 1) & 1
    return row, code & (col_blocks - 1)


def at_once(slots, most):
    return max(n for n in range(1, most + 1) if slots % n == 0)


def expand_body(code_ref, came, *rest, col_blocks):
    dense, (blocks, filled, arrival, leaving) = rest[:group], rest[group:]
    slots, size = came.shape[1], came.shape[2]
    several = at_once(slots, 8)
    order = list(reversed(range(group)))
    fetches = [
        pltpu.make_async_copy(came.at[place], blocks.at[place], arrival.at[place])
        for place in order
    ]
    stores = [
        pltpu.make_async_copy(filled.at[i % 2], dense[place], leaving.at[place])
        for i, place in enumerate(order)
    ]
    for fetch in fetches:
        fetch.start()
    for i, place in enumerate(order):
        if i >= 2:
            stores[i - 2].wait()
        rows_of = filled.at[i % 2]
        rows_of[...] = jnp.zeros_like(rows_of)
        fetches[i].wait()

        def some(first, carry):
            for j in range(several):
                slot = first * several + j
                code = code_ref[place * slots + slot]
                row, col = block_of(code, col_blocks)
                rows = pl.ds(pl.multiple_of(row * size, size), size)
                cols = pl.ds(pl.multiple_of((col & 1) * size, size), size)
                block = blocks[place, slot]
                block = jnp.where(code < 2 * col_blocks, block, jnp.zeros_like(block))
                rows_of[lax.shift_right_logical(col, 1), rows, cols] = block
            return carry

        lax.fori_loop(0, slots // several, some, 0)
        stores[i].start()
    for store in stores[-2:]:
        store.wait()


def expand(codes, weights, shards):
    width = 2 * weights.shape[2]
    hbm = pl.BlockSpec(memory_space=pltpu.HBM)
    return pl.pallas_call(
        functools.partial(expand_body, col_blocks=2 * shards),
        out_shape=(jax.ShapeDtypeStruct((shards, width, width), bf16),) * group,
        in_specs=[pl.BlockSpec(memory_space=pltpu.SMEM), hbm],
        out_specs=(hbm,) * group,
        scratch_shapes=[
            pltpu.VMEM(weights.shape, bf16),
            pltpu.VMEM((2, shards, width, width), bf16),
            pltpu.SemaphoreType.DMA((group,)),
            pltpu.SemaphoreType.DMA((group,)),
        ],
        compiler_params=params(44),
        name="expand",
    )(codes.reshape(-1), weights)


def layer_body(
    flags, gathered, own, above, above_own, above_scale, weight, here, inv_rms, gain, *rest,
    above_at, told, tell, phase,
):
    rest = list(rest)
    before = None if told else rest.pop(0)
    kept = rest.pop(0) if phase else None
    next_scale = rest.pop(0) if tell else None
    full_out, sent_out, own_out, kept_out = rest
    shards, width = weight.shape[0], weight.shape[1]
    tokens = own.shape[0]
    rows = slice(above_at * tokens, (above_at + 1) * tokens)

    if told:
        total = gathered[0, :, width:].astype(f32)
        for i in range(1, shards):
            total += gathered[i, :, width:].astype(f32)
    else:
        total = jnp.zeros((tokens, width), f32)
        for i in range(shards):
            change = gathered[i].astype(f32) - before[i].astype(f32)
            total += change * above[i, rows, :].astype(f32)
    if told:
        dots, scale = total[:, 0:1] + total[:, 1:2], own[:, width + 2:width + 3]
    else:
        dots, scale = jnp.sum(total, axis=1, keepdims=True), above_scale[...]
    factor = scale * dots

    acc = jnp.zeros((tokens, width), f32)
    for i in range(shards):
        piece = gathered[i, :, :width].astype(f32) - factor * above[i, rows, :].astype(f32)
        piece = piece.astype(bf16)
        full_out[i] = piece
        acc += lax.dot_general(piece, weight[i], across_last, preferred_element_type=f32)

    grad = own[:, :width] - factor * above_own[...].astype(f32)
    scaled = gain[...] * acc
    rms = inv_rms[...]
    result = grad + rms * scaled
    own_out[:, :width] = result
    if not tell:
        sent_out[...] = result.astype(bf16)
    if tell:
        dots = jnp.sum(scaled * (here[...].astype(f32) * rms), axis=1, keepdims=True)
        high = dots.astype(bf16).astype(f32)
        low = (dots - high).astype(bf16).astype(f32)
        lane = lax.broadcasted_iota(jnp.int32, (tokens, lanes), 1)
        tail = jnp.where(lane == 1, low, jnp.where(lane == 2, next_scale[...], 0.0))
        own_out[:, width:] = jnp.where(lane == 0, high, tail)
        sent_out[...] = own_out[...].astype(bf16)

    half = shards // 2
    mine = pl.ds(flags[0] * half, half)
    if phase:

        @pl.when(flags[phase] == 1)
        def _():
            kept_out[...] = full_out[mine]

        @pl.when(flags[phase] == 0)
        def _():
            kept_out[...] = kept[...]
    else:
        kept_out[...] = full_out[mine]


def layer(flags, operands, before, kept, next_scale, above_at, phase):
    weight, own = operands[5], operands[1]
    shards, width, tokens = weight.shape[0], weight.shape[1], own.shape[0]
    extra = [] if before is None else [before]
    extra += [] if kept is None else [kept]
    extra += [] if next_scale is None else [next_scale]
    tell = next_scale is not None
    wide = width + (lanes if tell else 0)
    vmem = pl.BlockSpec(memory_space=pltpu.VMEM)
    return pl.pallas_call(
        functools.partial(
            layer_body, above_at=above_at, told=before is None, tell=tell, phase=phase
        ),
        out_shape=(
            jax.ShapeDtypeStruct((shards, tokens, width), bf16),
            jax.ShapeDtypeStruct((tokens, wide), bf16),
            jax.ShapeDtypeStruct((tokens, wide), f32),
            jax.ShapeDtypeStruct((shards // 2, tokens, width), bf16),
        ),
        in_specs=[pl.BlockSpec(memory_space=pltpu.SMEM)] + [vmem] * (len(operands) + len(extra)),
        out_specs=(vmem,) * 4,
        compiler_params=params(12),
        name="layer",
    )(flags, *operands, *extra)


def grads_body(
    code_ref, mine, other, inputs, gain, blocks, out, gain_out, right, left, totals,
    *, col_blocks,
):
    size = blocks.shape[1]
    half, part = mine.shape[1] - 1, mine.shape[2]
    slots = blocks.shape[0]
    core = code_ref[slots]
    for x in range(group):
        rms = jnp.sum(mine[x, half].astype(f32), axis=1, keepdims=True)
        normed = (inputs[x].astype(f32) * rms * gain[...]).astype(bf16)
        right[0, x * part:(x + 1) * part, :] = normed[:, :size]
        right[1, x * part:(x + 1) * part, :] = normed[:, size:]
    for row in range(2):
        left[row] = right[row].astype(f32).T.astype(bf16)
        totals[row] = jnp.zeros_like(totals[row])

    def arrange(place, carry):
        for came, base in ((mine, core * half), (other, (1 - core) * half)):
            col = 2 * (base + place)
            for x in range(group):
                rows = slice(x * part, (x + 1) * part)
                right[col, rows, :] = came[x, place, :, :size]
                right[col + 1, rows, :] = came[x, place, :, size:]
        return carry

    lax.fori_loop(0, half, arrange, 0)
    dead = 2 * col_blocks
    several = at_once(slots, 4)

    def some(first, carry):
        found = []
        for i in range(several):
            code = code_ref[first * several + i]
            live = (code < dead).astype(f32)
            row, col = block_of(code, col_blocks)
            grad = jnp.dot(left[row], right[col], preferred_element_type=f32) * live
            found.append((row, grad))
        for i, (row, grad) in enumerate(found):
            slot = first * several + i
            out[slot] = grad.astype(bf16)
            totals[row] += grad * blocks[slot].astype(f32)
        return carry

    lax.fori_loop(0, slots // several, some, 0)
    for row in range(2):
        gain_out[row * size:(row + 1) * size, :] = jnp.sum(totals[row], axis=1, keepdims=True)


def slot_grads(codes, mine, other, inputs, gain, blocks):
    size = blocks.shape[1]
    parts, part, width = inputs.shape
    shards = 2 * (mine.shape[1] - 1)
    vmem = pl.BlockSpec(memory_space=pltpu.VMEM)
    return pl.pallas_call(
        functools.partial(grads_body, col_blocks=2 * shards),
        out_shape=(
            jax.ShapeDtypeStruct(blocks.shape, bf16),
            jax.ShapeDtypeStruct((width, 1), f32),
        ),
        in_specs=[pl.BlockSpec(memory_space=pltpu.SMEM)] + [vmem] * 5,
        out_specs=(vmem, vmem),
        scratch_shapes=[
            pltpu.VMEM((2 * shards, parts * part, size), bf16),
            pltpu.VMEM((2, size, parts * part), bf16),
            pltpu.VMEM((2, size, size), f32),
        ],
        compiler_params=params(32),
        name="slot_grads",
    )(codes, mine, other, inputs, gain, blocks)


def in_parts(value):
    parts = []
    for _ in range(3):
        part = lax.reduce_precision(value, 8, 7)
        parts.append(part.astype(bf16))
        value = value - part
    return parts


def per_device(x_saved, gains, w_blocks, slot_pos, slot_live, kl_grads, teacher):
    sections, shards = lax.axis_size("pipe"), lax.axis_size("tp")
    section, shard = lax.axis_index("pipe"), lax.axis_index("tp")
    line, block = section // group, section % group
    lines = sections // group
    together = [[i * group + x for x in range(group)] for i in range(lines)]
    down = [(i, i - group) for i in range(group, sections)]
    tokens, width = x_saved.shape[1], x_saved.shape[2]
    part = tokens // group
    full_width = width * shards
    blocks = w_blocks[0]
    slots = blocks.shape[0]
    places = 4 * shards
    codes = slot_pos[0] - shard * places + places * (1 - slot_live[0])

    code_row = jnp.zeros((width,), f32).at[:slots].set(codes.astype(f32)).astype(bf16)
    notes = jnp.stack(in_parts(gains[0]) + [code_row])
    notes = jnp.concatenate([notes, jnp.zeros((12, width), bf16)])
    notes = jnp.broadcast_to(notes[None], (group,) + notes.shape)
    told = jnp.concatenate([x_saved[0].reshape(group, part, width), notes], axis=1)
    told = lax.all_to_all(told, "pipe", 0, 0, axis_index_groups=together)
    inputs = told[:, :part]
    gain_rows = jnp.sum(told[:, part:part + 3].astype(f32), axis=1)
    line_codes = told[:, part + 3, :slots].astype(jnp.int32)

    first = group - 1
    upper_own = lax.ppermute(inputs[0], "pipe", down)
    weights = lax.all_gather(blocks, "pipe", axis_index_groups=together)
    second_inputs = lax.all_gather(inputs[first], "tp")

    partial = jnp.sum(jnp.square(inputs.astype(f32)), axis=2)
    partial = jnp.concatenate([p.T for p in in_parts(partial)], axis=1)
    partial = jnp.pad(partial, ((0, 0), (0, lanes - 3 * group)))
    entry = jnp.where((teacher == 1)[:, None], kl_grads[1], kl_grads[0])
    entry = lax.dynamic_slice_in_dim(entry, block * part, part, 0)
    own = jnp.pad(entry.astype(f32), ((0, 0), (0, lanes)))
    no_scale = jnp.zeros((part, 1), f32)
    sent = jnp.concatenate([entry, partial], axis=1)
    sent, second_inputs = lax.optimization_barrier((sent, second_inputs))
    gathered = lax.all_gather(sent, "tp")
    squares = jnp.sum(gathered[:, :, width:].astype(f32), axis=0)[:, :3 * group]
    squares = jnp.sum(squares.reshape(part, 3, group), axis=1).T
    inv_rms = lax.rsqrt(squares / full_width + norm_epsilon)[:, :, None]
    correct = jnp.square(inv_rms) / full_width

    third, gathered = lax.optimization_barrier((inputs[first - 1], gathered))
    third_inputs = lax.all_gather(third, "tp")
    weights, third_inputs = lax.optimization_barrier((weights, third_inputs))
    rest = jnp.concatenate([inputs[:first - 1].reshape(-1, width), upper_own])
    rest, weights = lax.optimization_barrier((rest, weights))
    rest_inputs = lax.all_gather(rest, "tp")

    found = {first: (second_inputs, 0), first - 1: (third_inputs, 0)}
    flags = [shard % 2] + [line == lines - 1 - phase for phase in range(1, lines)]
    flags = jnp.stack([flag.astype(jnp.int32) for flag in flags])
    dense = expand(line_codes, weights, shards)
    kept = [None] * group
    full = None
    for step in range(sections):
        phase, place = step // group, first - step % group
        before = full
        if step == 0:
            (above, above_at), above_own = found[first], inputs[first]
            scale = no_scale
        elif place == first:
            own = lax.ppermute(own, "pipe", down)
            sent, scale = own.astype(bf16), no_scale
            above, above_at, above_own = rest_inputs, 2, upper_own
            before = None
        else:
            (above, above_at), above_own = found[place + 1], inputs[place + 1]
            scale = correct[place + 1]
        if step > 0:
            gathered = lax.all_gather(sent, "tp")
        if step == 2:
            gathered, rest_inputs = lax.optimization_barrier((gathered, rest_inputs))
            found[1], found[0] = (rest_inputs, 1), (rest_inputs, 0)
        operands = (
            gathered, own, above, above_own, scale, dense[place],
            inputs[place], inv_rms[place], gain_rows[place][None],
        )
        next_scale = correct[0] if place == 0 and step < sections - 1 else None
        full, sent, own, kept[place] = layer(
            flags, operands, before, kept[place], next_scale, above_at, phase
        )

    rms_parts = jnp.concatenate(in_parts(inv_rms), axis=2)
    rms_parts = jnp.pad(rms_parts, ((0, 0), (0, 0), (0, width - 3)))
    leaving = jnp.concatenate([jnp.stack(kept), rms_parts[:, None]], axis=1)
    came = lax.all_to_all(leaving, "pipe", 0, 0, axis_index_groups=together)
    other = lax.ppermute(came, "tp", [(i, i ^ 1) for i in range(shards)])
    native = x_saved[0].reshape(group, part, width)
    codes = jnp.concatenate([codes, (shard % 2).astype(jnp.int32)[None]])
    w_grads, gain_sums = slot_grads(codes, came, other, native, gains, blocks)
    return (w_grads[None], gain_sums.reshape(1, width) / gains)


def solution(mesh):
    in_specs = (
        P("pipe", None, "tp"),
        P("pipe", "tp"),
        P("pipe", "tp", None, None),
        P("pipe", "tp"),
        P("pipe", "tp"),
        P(None, None, "tp"),
        P(),
    )
    out_specs = (P("pipe", "tp", None, None), P("pipe", "tp"))
    return jax.shard_map(
        per_device, mesh=mesh, in_specs=in_specs, out_specs=out_specs, check_vma=False
    )
```
